128 devices in a mesh: dp: 16 (over z_lo, x, core), ctx: 8 (over z_hi, y).
Axes of the slice: x: 4, y: 4, z: 4 (z_hi: 2, z_lo: 2; z = z_hi * 2 + z_lo), core: 2. Of those that a mesh axis runs over, the one named last changes fastest.
Arguments:
- inputs: bfloat16 [16, 1024, 1024], P('dp', 'ctx'), may hold values from -6 to 6
- out_grad: bfloat16 [16, 1024, 1024], P('dp', 'ctx'), may hold values from -6 to 6
- attn_weights: float32 [4, 1024, 1024], P(None, ('dp', 'ctx'))
- ffn_weights: float32 [2, 4096, 1024], P(None, ('dp', 'ctx'))
- vectors: float32 [13312], P(('dp', 'ctx'))
- attn_moment: float32 [4, 1024, 1024], P(None, ('dp', 'ctx'))
- ffn_moment: float32 [2, 4096, 1024], P(None, ('dp', 'ctx'))
- vec_first: float32 [13312], P(('dp', 'ctx'))
- vec_second: float32 [13312], P(('dp', 'ctx')), as said below
Outputs:
- outputs: bfloat16 [16, 1024, 1024], P('dp', 'ctx')
- input_grad: float32 [16, 1024, 1024], P('dp', 'ctx')
- attn_grad: float32 [4, 1024, 1024], P(None, ('dp', 'ctx'))
- ffn_grad: float32 [2, 4096, 1024], P(None, ('dp', 'ctx'))
- vec_grad: float32 [13312], P(('dp', 'ctx'))
- attn_moment_new: float32 [4, 1024, 1024], P(None, ('dp', 'ctx'))
- ffn_moment_new: float32 [2, 4096, 1024], P(None, ('dp', 'ctx'))
- attn_new: float32 [4, 1024, 1024], P(None, ('dp', 'ctx'))
- ffn_new: float32 [2, 4096, 1024], P(None, ('dp', 'ctx'))
- vec_first_new: float32 [13312], P(('dp', 'ctx'))
- vec_second_new: float32 [13312], P(('dp', 'ctx'))
- vec_new: float32 [13312], P(('dp', 'ctx'))
The draws below stay inside these ranges and needn't reach their ends.
Inputs may be any that keep to these rules, and one draw needn't show every extreme that they name: `vec_second`: entries are positive.
All inputs are finite; a program needn't handle non-finite values.
Results may differ from the reference program's by a relative error of at most 0.004.
The reference program's roundings to bfloat16 on the way count: a program that leaves them out, or rounds other values in their place, can miss the bound.
Values may be sent and summed in bfloat16 or wider, within the bound.
No kernel may reach another device: no remote copies, remote signals or barrier semaphores. Data moves between devices by JAX's collectives and lax.ppermute only.
A program may use at most 192 MiB of HBM per device.

```python
import math
import jax
import jax.numpy as jnp
from jax import lax

D = 1024
FF = 4096
HEADS = 16
HD = 64
ROT = 16
ITERS = 3
STEP = 10
LENGTH = 1024
SEQS = 16
N_DP = 16
N_CTX = 8


def row_profile(rows, peak):
    block_rows = rows // (N_DP * N_CTX)
    place = jnp.arange(rows) // block_rows % N_CTX
    ratio = place.astype(jnp.float32) / (N_CTX - 1)
    return (1.0 + (peak - 1.0) * ratio) / (0.5 * (1.0 + peak))


def draw_attn_weights(key, part):
    key = jax.random.fold_in(key, 11)
    noise = jax.random.normal(key, (4, D, D), jnp.float32)
    spreads = jnp.array([1.45 * D ** (-0.5), 1.45 * D ** (-0.5), D ** (-0.5), 2.0 * D ** (-0.5)], jnp.float32)
    return noise * spreads[:, None, None]


def draw_ffn_weights(key, part):
    key = jax.random.fold_in(key, 12)
    noise = jax.random.normal(key, (2, FF, D), jnp.float32)
    spreads = jnp.array([D ** (-0.5), 2.0 * FF ** (-0.5)], jnp.float32)
    return noise * spreads[:, None, None]


def draw_vectors(key, part):
    key = jax.random.fold_in(key, 13)
    noise = jax.random.normal(key, (9 * D + FF,), jnp.float32)
    segment = jnp.arange(9 * D + FF) // D
    is_gain = (segment == 0) | (segment == 2)
    return jnp.where(is_gain, 1.0 + 0.15 * noise, 0.2 * noise)


def draw_attn_moment(key, part):
    key = jax.random.fold_in(key, 14)
    noise = jax.random.normal(key, (4, D, D), jnp.float32)
    peak = 6.0
    spreads = jnp.array([0.4, 0.4, 0.6, 0.4], jnp.float32) * math.sqrt(SEQS * LENGTH)
    return noise * spreads[:, None, None] * row_profile(D, peak)[None, :, None]


def draw_ffn_moment(key, part):
    key = jax.random.fold_in(key, 15)
    noise = jax.random.normal(key, (2, FF, D), jnp.float32)
    peak = 6.0
    spreads = jnp.array([0.6, 0.65], jnp.float32) * math.sqrt(SEQS * LENGTH)
    return noise * spreads[:, None, None] * row_profile(FF, peak)[None, :, None]


def draw_vec_first(key, part):
    key = jax.random.fold_in(key, 16)
    noise = jax.random.normal(key, (9 * D + FF,), jnp.float32)
    return noise * (0.111 * 2.0 * math.sqrt(SEQS * LENGTH))


def draw_vec_second(key, part):
    key = jax.random.fold_in(key, 18)
    spread = jax.random.uniform(key, (9 * D + FF,), jnp.float32, 0.0, math.log(4.0))
    return jnp.exp(spread) * (0.0526 * 4.0 * SEQS * LENGTH)


def steps_of(stream_key, dims, shards, smallest, top_value):
    loudness, own = 1.0, jax.random.fold_in(stream_key, 6)
    for dim, blocks in shards:
        draws = jnp.exp(jax.random.uniform(jax.random.fold_in(own, dim), (blocks,), jnp.float32, smallest / len(shards), top_value / len(shards)))
        loudness = loudness * jnp.repeat(draws, dims[dim] // blocks).reshape([-1 if axis == dim else 1 for axis in range(len(dims))])
    return loudness


def scatter_about(rng, extent, scale, limit, split=(), dtype=jnp.bfloat16):
    loudness = steps_of(rng, extent, split, -0.22, 0.18) if split else 1.0
    values = jax.random.normal(rng, extent, jnp.float32) * scale * loudness
    return jnp.minimum(jnp.maximum(values, -limit), limit).astype(dtype)


def setup_inputs(seed: int = 0) -> dict:
    key_list = jax.random.split(jax.random.key(seed), 10)
    return {
        "inputs": scatter_about(key_list[0], (SEQS, LENGTH, D), 1.0, 6.0, ((0, 16), (1, 8))),
        "out_grad": scatter_about(key_list[1], (SEQS, LENGTH, D), 1.0, 6.0, ((0, 16), (1, 8))),
        "attn_weights": draw_attn_weights(jax.random.fold_in(key_list[9], 71), 0),
        "ffn_weights": draw_ffn_weights(jax.random.fold_in(key_list[9], 71), 0),
        "vectors": draw_vectors(jax.random.fold_in(key_list[9], 71), 0),
        "attn_moment": draw_attn_moment(jax.random.fold_in(key_list[9], 71), 0),
        "ffn_moment": draw_ffn_moment(jax.random.fold_in(key_list[9], 71), 0),
        "vec_first": draw_vec_first(jax.random.fold_in(key_list[9], 71), 0),
        "vec_second": draw_vec_second(jax.random.fold_in(key_list[9], 71), 0),
    }


norm_epsilon = 1e-05
quintic_one = 3.4445
quintic_two = -4.775
quintic_three = 2.0315
momentum_decay = 0.95
learn_rate = 0.4
weight_decay = 0.01
beta_first = 0.9
beta_second = 0.95
vector_rate = 0.05
adam_epsilon = 1e-08
highest = lax.Precision.HIGHEST

@jax.custom_vjp
def low(v):
    return lax.optimization_barrier(v.astype(jnp.bfloat16)).astype(jnp.float32)

@jax.custom_vjp
def low_back(v):
    return v

def low_keep(v):
    return (low(v), None)

def low_pass(kept, grad):
    return (grad,)

def back_keep(v):
    return (v, None)

def back_low(kept, grad):
    return (low(grad),)
low.defvjp(low_keep, low_pass)
low_back.defvjp(back_keep, back_low)

def rope_tables(positions):
    half_rot = ROT // 2
    inv_freq = 10000.0 ** (-(jnp.arange(half_rot).astype(jnp.float32) * 2.0) / ROT)
    angles = positions.astype(jnp.float32)[:, None] * inv_freq[None, :]
    angles = jnp.concatenate([angles, angles], axis=-1)
    return (jnp.cos(angles), jnp.sin(angles))

def rotate(tensor, cosines, sines):
    half_rot = ROT // 2
    part = tensor[..., :ROT]
    turned = jnp.concatenate([-part[..., half_rot:], part[..., :half_rot]], axis=-1)
    spun = part * cosines[:, None, :] + turned * sines[:, None, :]
    return jnp.concatenate([spun, tensor[..., ROT:]], axis=-1)

def orthogonalize(moment):
    mom_low = lax.optimization_barrier(moment.astype(jnp.bfloat16))
    mom_wide = mom_low.astype(jnp.float32)
    norm_value = jnp.sqrt(jnp.sum(mom_wide * mom_wide))
    current = (mom_wide / (norm_value + 1e-07)).astype(jnp.bfloat16)
    for repeat in range(ITERS):
        gram = jnp.dot(current.T, current, preferred_element_type=jnp.float32)
        gram_low = gram.astype(jnp.bfloat16)
        square = jnp.dot(gram_low, gram_low, preferred_element_type=jnp.float32)
        mixer = (quintic_two * gram + quintic_three * square).astype(jnp.bfloat16)
        current = (quintic_one * current.astype(jnp.float32) + jnp.dot(current, mixer, preferred_element_type=jnp.float32)).astype(jnp.bfloat16)
    return current.astype(jnp.float32)

def reference(inputs, out_grad, attn_weights, ffn_weights, vectors, attn_moment, ffn_moment, vec_first, vec_second):
    inputs_wide = inputs.astype(jnp.float32)
    cotangent = out_grad.astype(jnp.float32)
    positions = jnp.arange(LENGTH)
    cosines, sines = rope_tables(positions)
    causal = positions[:, None] >= positions[None, :]
    scale = HD ** (-0.5)

    def layer(x_all, attn_w, ffn_w, vec_w):
        attn_l = low(attn_w)
        ffn_l = low(ffn_w)
        vec_l = low(vec_w)
        pieces = [vec_l[index * D:(index + 1) * D] for index in range(9)]
        gain_one, bias_one, gain_two, bias_two, bias_q, bias_k, bias_v, bias_o, bias_down = pieces
        bias_up = vec_l[9 * D:]

        def one_seq(x_seq):
            mean_value = lax.optimization_barrier(jnp.mean(x_seq, axis=-1, keepdims=True))
            centered = x_seq - mean_value
            var_value = lax.optimization_barrier(jnp.mean(centered * centered, axis=-1, keepdims=True))
            normed = centered * lax.rsqrt(var_value + norm_epsilon)
            first_in = low(normed * gain_one + bias_one)
            second_in = low(normed * gain_two + bias_two)
            query = low_back(jnp.dot(first_in, attn_l[0], precision=highest) + bias_q)
            key_pre = low_back(jnp.dot(first_in, attn_l[1], precision=highest) + bias_k)
            value = low_back(jnp.dot(first_in, attn_l[2], precision=highest) + bias_v)
            q_rot = low(rotate(query.reshape(LENGTH, HEADS, HD), cosines, sines))
            k_rot = low(rotate(key_pre.reshape(LENGTH, HEADS, HD), cosines, sines))
            v_low = low(value.reshape(LENGTH, HEADS, HD))
            raw = low_back(jnp.einsum('qhd,khd->hqk', q_rot, k_rot, precision=highest))
            scores = jnp.where(causal[None], raw * scale, -1e+30)
            probs = low(jax.nn.softmax(scores, axis=-1))
            mixed = jnp.einsum('hqk,khd->qhd', probs, v_low, precision=highest).reshape(LENGTH, D)
            mixed = low(low_back(mixed))
            attn_branch = jnp.dot(mixed, attn_l[3], precision=highest) + bias_o
            up_pre = low_back(jnp.dot(second_in, ffn_l[0].T, precision=highest) + bias_up)
            hidden = low(jax.nn.gelu(up_pre, approximate=False))
            ffn_branch = jnp.dot(hidden, ffn_l[1], precision=highest) + bias_down
            return x_seq + attn_branch + ffn_branch
        return lax.map(jax.checkpoint(one_seq), x_all)
    result, pull = jax.vjp(layer, inputs_wide, attn_weights, ffn_weights, vectors)
    input_grad, attn_grad, ffn_grad, vec_grad = pull(cotangent)
    outputs = result.astype(jnp.bfloat16)
    attn_moment_new = momentum_decay * attn_moment + attn_grad
    ffn_moment_new = momentum_decay * ffn_moment + ffn_grad
    ortho_attn = jnp.stack([orthogonalize(attn_moment_new[index]) for index in range(4)])
    ortho_ffn = jnp.stack([orthogonalize(ffn_moment_new[index]) for index in range(2)])
    attn_steps = jnp.array([1.0, 1.0, 1.0, 2.0], jnp.float32)
    ffn_steps = jnp.array([(FF / D) ** 0.5, 2.0], jnp.float32)
    attn_new = attn_weights * (1.0 - learn_rate * weight_decay) - learn_rate * attn_steps[:, None, None] * ortho_attn
    ffn_new = ffn_weights * (1.0 - learn_rate * weight_decay) - learn_rate * ffn_steps[:, None, None] * ortho_ffn
    vec_first_new = beta_first * vec_first + (1.0 - beta_first) * vec_grad
    vec_second_new = beta_second * vec_second + (1.0 - beta_second) * vec_grad * vec_grad
    first_hat = vec_first_new / (1.0 - beta_first ** STEP)
    second_hat = vec_second_new / (1.0 - beta_second ** STEP)
    vec_new = vectors - vector_rate * first_hat / (jnp.sqrt(second_hat) + adam_epsilon)
    return (outputs, input_grad, attn_grad, ffn_grad, vec_grad, attn_moment_new, ffn_moment_new, attn_new, ffn_new, vec_first_new, vec_second_new, vec_new)
```

```python
import math

import jax
import jax.numpy as jnp
from jax import lax
from jax.experimental import pallas as pl
from jax.experimental.pallas import tpu as pltpu
from jax.sharding import Mesh
from jax.sharding import PartitionSpec as P

D = 1024
FF = 4096
HEADS = 16
HD = 64
ROT = 16
ITERS = 3
STEP = 10


norm_epsilon = 1e-05
quintic_one = 3.4445
quintic_two = -4.775
quintic_three = 2.0315
momentum_decay = 0.95
learn_rate = 0.4
weight_decay = 0.01
beta_first = 0.9
beta_second = 0.95
vector_rate = 0.05
adam_epsilon = 1e-08

low_type = jnp.bfloat16
wide_type = jnp.float32
dp_axes = ("z_lo", "x", "core")
ctx_axes = ("z_hi", "y")
chip_axes = ("z_lo", "x")
ffn_owners = (0, 6)
attn_owners = (1, 3, 5, 7)


def trade(blocks, axes):
    return lax.all_to_all(blocks, axes, split_axis=0, concat_axis=0, tiled=True)


def spread(block, axes):
    return trade(jnp.broadcast_to(block, (lax.axis_size(axes),) + block.shape), axes)


def collect(partials, axes):
    return jnp.sum(trade(partials.astype(low_type), axes).astype(wide_type), axis=0)


def swap(block):
    return lax.ppermute(block, "core", [(0, 1), (1, 0)])


def halve(pairs):
    core = lax.axis_index("core")
    kept = lax.dynamic_index_in_dim(pairs, core, axis=0, keepdims=False)
    given = lax.dynamic_index_in_dim(pairs, 1 - core, axis=0, keepdims=False)
    return kept.astype(wide_type) + swap(given).astype(wide_type)


def pair(mine, other):
    first = lax.axis_index("core") == 0
    return jnp.stack([jnp.where(first, mine, other), jnp.where(first, other, mine)])


def split_low(wide):
    high = lax.reduce_precision(wide, 8, 7)
    return high.astype(low_type), (wide - high).astype(low_type)


def dot(left, right):
    return jnp.dot(left, right, preferred_element_type=wide_type)


def dot_nt(left, right):
    return lax.dot_general(
        left, right, (((1,), (1,)), ((), ())), preferred_element_type=wide_type
    )


def dot_tn(left, right):
    return lax.dot_general(
        left, right, (((0,), (0,)), ((), ())), preferred_element_type=wide_type
    )


def rope_tables(length, heads):
    lane = lax.rem(jnp.arange(heads * HD, dtype=jnp.int32), HD)
    half_rot = ROT // 2
    inv_freq = 10000.0 ** (-(lax.rem(lane, half_rot).astype(wide_type) * 2.0) / ROT)
    angles = jnp.arange(length, dtype=jnp.int32).astype(wide_type)[:, None] * inv_freq[None, :]
    keep = jnp.where(lane < ROT, jnp.cos(angles), 1.0)
    sines = jnp.sin(angles)
    ahead = jnp.where(lane < half_rot, -sines, 0.0)
    behind = jnp.where((lane >= half_rot) & (lane < ROT), sines, 0.0)
    return keep, ahead, behind


def turned(rows, tables):
    half_rot = ROT // 2
    cols = rows.shape[1]
    ahead = pltpu.roll(rows, cols - half_rot, 1)
    behind = pltpu.roll(rows, half_rot, 1)
    return ahead * tables[1] + behind * tables[2]


def attention_kernel(
    flags_ref, qkv_ref, mixed_grad_ref, keep_ref, ahead_ref, behind_ref, first_far, dy_far, mixed_ref, grad_ref, g_kept_ref,
    g_given_ref, k_sum, v_sum, g_all, first_ref, dy_ref, sems
):
    length, cols = keep_ref.shape
    heads = cols // HD
    scale = HD ** (-0.5)
    tables = (keep_ref[...], ahead_ref[...], behind_ref[...])
    first_copy = pltpu.make_async_copy(first_far, first_ref, sems.at[0])
    dy_copy = pltpu.make_async_copy(dy_far, dy_ref, sems.at[1])
    first_copy.start()
    dy_copy.start()
    q_rot = qkv_ref[:, :cols]
    k_rot = qkv_ref[:, cols : 2 * cols]
    v_low = qkv_ref[:, 2 * cols :]
    k_sum[...] = jnp.zeros_like(k_sum)
    v_sum[...] = jnp.zeros_like(v_sum)
    block = 256
    for start in range(0, length, block):
        stop = start + block
        q_grads = []
        for head in range(heads):
            lanes = slice(head*HD, (head+1)*HD)
            q_now, k_now, v_now = q_rot[start:stop, lanes], k_rot[:stop, lanes], v_low[:stop, lanes]
            grad_t = mixed_grad_ref[lanes, start:stop]
            raw = dot_nt(k_now, q_now) * scale
            key_pos = lax.broadcasted_iota(jnp.int32, (stop, block), 0)
            query_pos = lax.broadcasted_iota(jnp.int32, (stop, block), 1) + start
            scores = jnp.where(key_pos <= query_pos, raw, -1e30)
            expo = jnp.exp(scores - jnp.max(scores, axis=0, keepdims=True))
            probs = expo * (1.0 / jnp.sum(expo, axis=0, keepdims=True))
            probs_low = probs.astype(low_type)
            mixed_ref[lanes, start:stop] = dot_tn(v_now, probs_low).astype(low_type)
            grad_probs = dot(v_now, grad_t)
            inner = jnp.sum(probs * grad_probs, axis=0, keepdims=True)
            grad_raw = (probs * (grad_probs - inner) * scale).astype(low_type)
            q_grads.append(dot_tn(k_now, grad_raw))
            k_sum[head, :stop, :] += dot(grad_raw, q_now)
            v_sum[head, :stop, :] += dot_nt(probs_low, grad_t)
        grad_q = jnp.concatenate(q_grads, axis=0).T
        part = tuple(table[start:stop] for table in tables)
        grad_ref[start:stop, :cols] = (grad_q * part[0] - turned(grad_q, part)).astype(low_type)
    grad_k = jnp.concatenate([k_sum[head] for head in range(heads)], axis=1)
    grad_v = jnp.concatenate([v_sum[head] for head in range(heads)], axis=1)
    grad_ref[:, cols:2*cols] = (grad_k * tables[0] - turned(grad_k, tables)).astype(low_type)
    grad_ref[:, 2*cols:] = grad_v.astype(low_type)
    first_copy.wait()
    dy_copy.wait()
    for start in range(0, first_ref.shape[1], block):
        g_all[start : start + block, : 3 * cols] = dot_tn(
            first_ref[:, start : start + block], grad_ref[...]
        ).astype(low_type)
        g_all[start : start + block, 3 * cols :] = dot(
            mixed_ref[...], dy_ref[:, start : start + block]
        ).T.astype(low_type)
    chips, part = g_kept_ref.shape[:2]
    core = flags_ref[0]
    for chip in range(chips):
        for place, out_ref in ((core, g_kept_ref), (1 - core, g_given_ref)):
            out_ref[chip] = g_all[pl.ds(pl.multiple_of((2 * chip + place) * part, part), part)]


def vmem_specs(count):
    return [pl.BlockSpec(memory_space=pltpu.VMEM)] * count


def call(kernel, outs, args, flops, scratch=(), flags=None, name=None, views={}, far=(), far_out=()):
    specs, size = [], 0
    for index, each in enumerate(args):
        block, place = views.get(index, (each.shape, (0,) * each.ndim))
        if index in far:
            specs.append(pl.BlockSpec(memory_space=pl.ANY))
        else:
            specs.append(pl.BlockSpec(block, lambda step, place=place: place))
        size += math.prod(block) * each.dtype.itemsize
    size += sum(math.prod(each.shape) * each.dtype.itemsize for each in outs)
    args = list(args)
    if flags is not None:
        specs = [pl.BlockSpec(memory_space=pltpu.SMEM)] + specs
        args = [jnp.stack([jnp.asarray(flag, jnp.int32) for flag in flags])] + args
    return pl.pallas_call(
        kernel,
        grid=(1,),
        out_shape=tuple(outs),
        in_specs=specs,
        out_specs=tuple(
            pl.BlockSpec(memory_space=pl.ANY)
            if index in far_out
            else pl.BlockSpec(each.shape, lambda step, rank=len(each.shape): (0,) * rank)
            for index, each in enumerate(outs)
        ),
        scratch_shapes=list(scratch),
        compiler_params=pltpu.CompilerParams(vmem_limit_bytes=60 * 1024 * 1024),
        cost_estimate=pl.CostEstimate(flops=flops, bytes_accessed=size, transcendentals=0),
        name=name,
    )(*args)


def wide(*shape):
    return jax.ShapeDtypeStruct(shape, wide_type)


def low(*shape):
    return jax.ShapeDtypeStruct(shape, low_type)


def normalized(rows):
    rows = rows.astype(wide_type)
    centered = rows - jnp.mean(rows, axis=-1, keepdims=True)
    variance = jnp.mean(centered * centered, axis=-1, keepdims=True)
    return centered * lax.rsqrt(variance + norm_epsilon)


def pack_kernel(x_ref, weights_ref, moment_ref, vec_ref, out_ref):
    tokens = x_ref.shape[0]
    cols = weights_ref.shape[2] // out_ref.shape[0]
    for target in range(out_ref.shape[0]):
        lanes = slice(target * cols, (target + 1) * cols)
        out_ref[target, :tokens] = x_ref[...]
        vec = jnp.broadcast_to(vec_ref[...], (weights_ref.shape[1], vec_ref.shape[1]))
        weights = [weights_ref[index, :, lanes] for index in range(4)]
        blank = jnp.zeros((weights_ref.shape[1], 4 * cols - vec_ref.shape[1]), wide_type)
        moments = [moment_ref[index, :, lanes] for index in range(3)]
        highs = [moment.astype(low_type).astype(wide_type) for moment in moments]
        lows = [moment - high for moment, high in zip(moments, highs)]
        rest = jnp.zeros((weights_ref.shape[1], 2 * cols), wide_type)
        upper = jnp.concatenate([*weights, vec, blank], axis=1)
        lower = jnp.concatenate([*highs, *lows, rest], axis=1)
        out_ref[target, tokens:] = jnp.concatenate([upper, lower], axis=0).astype(low_type)


def owners_kernel(ffn_moment_ref, ffn_grad_ref, moment_ref, grad_ref, out_ref, ffn_new_ref):
    for index, owner in enumerate(ffn_owners):
        rows = momentum_decay * ffn_moment_ref[index] + ffn_grad_ref[index]
        ffn_new_ref[index] = rows
        out_ref[owner] = rows.astype(low_type)
    block = momentum_decay * moment_ref[...] + grad_ref[...]
    cols, rows = block.shape[1] // 4, 8
    groups = block.shape[0] // rows
    blank = jnp.zeros((out_ref.shape[1] - rows, out_ref.shape[2]), wide_type)
    for index, owner in enumerate(attn_owners):
        lanes = slice(index * cols, (index + 1) * cols)
        parts = [block[rows * group : rows * (group + 1), lanes] for group in range(groups)]
        filled = jnp.concatenate([jnp.concatenate(parts, axis=1), blank], axis=0)
        out_ref[owner] = filled.astype(low_type)
    for owner in range(out_ref.shape[0]):
        if owner not in ffn_owners + attn_owners:
            out_ref[owner] = jnp.zeros(out_ref.shape[1:], low_type)


def unpack_kernel(flags_ref, mine_ref, other_ref, dy_ref, qkv_ref, out_ref):
    half, tokens, cols = 32, dy_ref.shape[0], out_ref.shape[2] // 8
    first = flags_ref[0] == 0
    mine, other = mine_ref[:, :half], other_ref[:, :half]
    for core, part in enumerate((jnp.where(first, mine, other), jnp.where(first, other, mine))):
        for upper in range(2):
            lanes = part[:, :, upper * 4 * cols : (upper + 1) * 4 * cols]
            qkv_ref[:, core, upper * half : (upper + 1) * half] = lanes[:, :, : 3 * cols]
            for group in range(2):
                place = (4 * core + 2 * upper + group) * cols
                out_ref[:, tokens : tokens + 16, place : place + cols] = lanes[
                    :, 16 * group : 16 * (group + 1), 3 * cols :
                ]
    rows = []
    for ref in (mine_ref, other_ref):
        last = ref[:, half:].astype(wide_type)
        rows.append(jnp.where(first, last[:, 1:2], last[:, 2:3]))
    blank = jnp.zeros((out_ref.shape[0], 14, out_ref.shape[2]), wide_type)
    pair_rows = [jnp.where(first, rows[0], rows[1]), jnp.where(first, rows[1], rows[0])]
    out_ref[:, tokens + 16 :] = jnp.concatenate([*pair_rows, blank], axis=1).astype(low_type)
    for target in range(out_ref.shape[0]):
        out_ref[target, :tokens] = dy_ref[...]


def qkv_kernel(
    x_ref, keep_ref, ahead_ref, behind_ref, gain_ref, shift_ref, w_ref, bias_ref, first_ref, out_ref
):
    cols = keep_ref.shape[1]
    tables = (keep_ref[...], ahead_ref[...], behind_ref[...])
    normed = normalized(x_ref[...].reshape(first_ref.shape))
    first = (normed * gain_ref[...] + shift_ref[...]).astype(low_type)
    first_ref[...] = first
    rows = dot(first, w_ref[...]) + bias_ref[...]
    for index in range(2):
        part = rows[:, index * cols : (index + 1) * cols]
        out_ref[:, index * cols : (index + 1) * cols] = (
            part * tables[0] + turned(part, tables)
        ).astype(low_type)
    out_ref[:, 2 * cols :] = rows[:, 2 * cols :].astype(low_type)


def ffn_forward_kernel(x_ref, gain_ref, shift_ref, up_ref, bias_ref, second_ref, hidden_ref, slope_ref):
    sources, tokens, width = x_ref.shape
    for source in range(sources):
        second_ref[source * tokens : (source + 1) * tokens] = (
            normalized(x_ref[source]) * gain_ref[...] + shift_ref[...]
        ).astype(low_type)
    for index in range(2):
        pre = dot_nt(up_ref[:, index].reshape(-1, width), second_ref[...]) + bias_ref[index]
        chance = 0.5 * (1.0 + lax.erf(pre * math.sqrt(0.5)))
        density = jnp.exp(-0.5 * pre * pre) * (1.0 / math.sqrt(2.0 * math.pi))
        hidden_ref[index] = (pre * chance).astype(low_type)
        slope_ref[index] = chance + pre * density


def ffn_backward_kernel(
    flags_ref, pack_ref, rows_ref, slope_ref, second_ref, hidden_ref, dy_ref, grad_up_ref, kept_ref,
    given_ref, g_bias_ref, w_out_ref, mixed_grad_ref, dy, down, slope, second, hidden, out_rows, sems
):
    chips, units, width = kept_ref.shape
    units = units // 2
    sources, tokens = pack_ref.shape[0], pack_ref.shape[1] - 32
    copies = []

    def fetch(source, target):
        copy = pltpu.make_async_copy(source, target, sems.at[len(copies)])
        copy.start()
        copies.append(copy)
        return copy

    parts = []
    for source in range(sources):
        parts.append(
            fetch(pack_ref.at[source, pl.ds(0, tokens)], dy.at[pl.ds(source * tokens, tokens)])
        )
    parts.append(fetch(rows_ref.at[:, :, pl.ds(units, units)], down))
    slope_copy = fetch(slope_ref, slope)
    second_copy = fetch(second_ref, second)
    hidden_copy = fetch(hidden_ref, hidden)
    out_copy = fetch(pack_ref.at[:, pl.ds(tokens, 16)], out_rows)
    for part in parts:
        part.wait()
    back_copy = fetch(dy, dy_ref)
    ones = jnp.ones((8, dy.shape[0]), low_type)
    for index in range(2):
        grad_hidden = dot_nt(down[:, index].reshape(-1, width), dy[...])
        if index == 0:
            slope_copy.wait()
        grad_up = (grad_hidden * slope[index]).astype(low_type)
        grad_up_ref[index] = grad_up
        g_bias_ref[index] = dot_nt(ones, grad_up)
        if index == 0:
            second_copy.wait()
        g_up = dot(grad_up, second[...]).astype(low_type).reshape(chips, units, width)
        if index == 0:
            hidden_copy.wait()
        g_down = dot(hidden[index], dy[...]).astype(low_type).reshape(chips, units, width)

        @pl.when(flags_ref[0] == index)
        def _():
            kept_ref[:, :units] = g_up
            kept_ref[:, units:] = g_down

        @pl.when(flags_ref[0] != index)
        def _():
            given_ref[:, :units] = g_up
            given_ref[:, units:] = g_down

    out_copy.wait()
    cols = width // sources
    for source in range(sources):
        for group in range(8):
            w_out_ref[16 * group : 16 * (group + 1), source * cols : (source + 1) * cols] = out_rows[
                source, :, group * cols : (group + 1) * cols
            ]
    mixed_grad_ref[...] = dot_nt(w_out_ref[...], dy[...]).astype(low_type)
    back_copy.wait()


def normal_kernel(
    grad_ref, grad_up_ref, x_ref, w_ref, rows_ref, gain_one_ref, gain_two_ref, out_ref, sums_ref
):
    first = dot_nt(grad_ref[...], w_ref[...])
    second = 0.0
    for index in range(2):
        up = rows_ref[:, index].reshape(-1, first.shape[1])
        second = second + dot_tn(grad_up_ref[index], up)
    normed = normalized(x_ref[...].reshape(first.shape))
    out_ref[...] = (first * gain_one_ref[...] + second * gain_two_ref[...]).astype(low_type)
    terms = (first * normed, first, second * normed, second)
    sums = jnp.concatenate([jnp.sum(term, axis=0, keepdims=True) for term in terms], axis=0)

    @pl.when(pl.program_id(0) == 0)
    def _():
        sums_ref[...] = jnp.zeros_like(sums_ref)

    sums_ref[...] += sums


def branch_kernel(hidden_ref, mixed_ref, rows_ref, w_out_ref, out_ref):
    total = dot_tn(mixed_ref[...], w_out_ref[...])
    for index in range(2):
        down = rows_ref[:, index].reshape(-1, total.shape[1])
        total = total + dot_tn(hidden_ref[index], down)
    out_ref[...] = total


def gram_kernel(flags_ref, own_ref, other_ref, out_ref):
    half, cols = out_ref.shape[1:]
    lanes = pl.ds(pl.multiple_of(flags_ref[0] * half, half), half)
    rows = dot_tn(own_ref[:, lanes], own_ref[...]) + dot_tn(other_ref[:, lanes], other_ref[...])
    for index in range(out_ref.shape[0]):
        out_ref[index] = rows[:, index * cols : (index + 1) * cols].astype(low_type)


def call_rows(kernel, outs, args, blocks, flops, steps, name):
    arrays = list(args) + list(outs)
    specs, size = [], 0
    for each, given in zip(arrays, blocks):
        shape, place = given or (each.shape, lambda step, rank=len(each.shape): (0,) * rank)
        specs.append(pl.BlockSpec(shape, place))
        size += math.prod(shape) * each.dtype.itemsize * (steps if given else 1)
    return pl.pallas_call(
        kernel,
        grid=(steps,),
        out_shape=tuple(outs),
        in_specs=specs[: len(args)],
        out_specs=tuple(specs[len(args) :]),
        compiler_params=pltpu.CompilerParams(vmem_limit_bytes=60 * 1024 * 1024),
        cost_estimate=pl.CostEstimate(flops=flops, bytes_accessed=size, transcendentals=0),
        name=name,
    )(*args)


def newton_schulz_kernel(
    flags_ref, mine_ref, other_ref, rows_ref, out_ref, gram_ref, low_ref, mixer_ref, start_ref, current_ref
):
    width = rows_ref.shape[1]
    half = width // 2
    block = 512
    chips = 8
    attn_rows, units = 8, rows_ref.shape[0] // chips
    core, ctx = flags_ref[1], flags_ref[2]
    cols = mine_ref.shape[2]
    part = half // chips

    @pl.when(flags_ref[0] == 1)
    def _():
        for source in range(mine_ref.shape[0]):
            lanes = slice(source * cols, (source + 1) * cols)
            for place, ref in ((core, mine_ref), (1 - core, other_ref)):
                rows = pl.ds(pl.multiple_of(place * half, half), half)
                gram_ref[rows, lanes] = ref[source, :half].astype(wide_type)
        total = jnp.zeros((1, 1), wide_type)
        for start in range(0, width, 256):
            square = gram_ref[start : start + 256, start : start + 256]
            diagonal = lax.broadcasted_iota(jnp.int32, square.shape, 0) == lax.broadcasted_iota(
                jnp.int32, square.shape, 1
            )
            total = total + jnp.sum(jnp.where(diagonal, square, 0.0), keepdims=True)
        factor = 1.0 / (jnp.sqrt(total) + 1e-07)
        gram_ref[...] = gram_ref[...] * (factor * factor)
        current_ref[...] = rows_ref[...].astype(wide_type) * factor

    @pl.when(flags_ref[0] == 0)
    def _():
        for source in range(mine_ref.shape[0]):
            lanes = slice(source * cols, (source + 1) * cols)
            for chip in range(chips):
                for place, ref in ((core, mine_ref), (1 - core, other_ref)):
                    rows = pl.ds(pl.multiple_of((2 * chip + place) * part, part), part)
                    gram_ref[rows, lanes] = ref[source, chip * part : (chip + 1) * part].astype(wide_type)
        raw = gram_ref[...]
        factor = 1.0 / (jnp.sqrt(jnp.sum(raw * raw, keepdims=True)) + 1e-07)
        start_ref[...] = (raw * factor).astype(low_type)
        blank = jnp.zeros((units - attn_rows, width), wide_type)
        for chip in range(chips):
            place = pl.multiple_of((2 * chip + core) * part + attn_rows * ctx, attn_rows)
            rows = gram_ref[pl.ds(place, attn_rows)] * factor
            current_ref[units * chip : units * (chip + 1)] = jnp.concatenate([rows, blank])

        @pl.when(flags_ref[3] == 1)
        def _():
            row = lax.broadcasted_iota(jnp.int32, current_ref.shape, 0)
            inner = lax.rem(row, units)
            place = (lax.div(row, units) * 2 + core) * part + attn_rows * ctx + inner
            lane = lax.broadcasted_iota(jnp.int32, current_ref.shape, 1)
            current_ref[...] = jnp.where((lane == place) & (inner < attn_rows), 1.0, 0.0)

        for start in range(0, width, 256):
            lanes = slice(start, start + 256)
            gram_ref[lanes] = dot_tn(start_ref[:, lanes], start_ref[...])

    def mix(index, carry):
        rows = pl.ds(pl.multiple_of(index * block, block), block)
        square = dot(low_ref[rows], low_ref[...])
        mixer_ref[rows] = (quintic_two * gram_ref[rows] + quintic_three * square).astype(low_type)
        return carry

    def advance(index, carry):
        rows = pl.ds(pl.multiple_of(index * block, block), block)
        turn = quintic_one * gram_ref[rows] + dot(low_ref[rows], mixer_ref[...])
        gram_ref[rows] = quintic_one * turn + dot(turn.astype(low_type), mixer_ref[...])
        return carry

    def times(rows, matrix_ref):
        return dot(rows.astype(low_type), matrix_ref[...])

    def factor_times(rows):
        return quintic_one * rows + times(rows, mixer_ref)

    for repeat in range(2):
        low_ref[...] = gram_ref[...].astype(low_type)
        lax.fori_loop(0, width // block, mix, 0)
        current_ref[...] = factor_times(current_ref[...])
        if repeat == 0:
            lax.fori_loop(0, width // block, advance, 0)

    def third_gram_times(rows):
        return factor_times(times(factor_times(rows), low_ref))

    current = current_ref[...]
    once = third_gram_times(current)
    twice = third_gram_times(once)
    current_ref[...] = quintic_one * current + quintic_two * once + quintic_three * twice
    out_ref[...] = current_ref[...].astype(low_type)

    @pl.when(flags_ref[3] == 1)
    def _():
        out_ref[...] = dot_nt(out_ref[...], start_ref[...]).astype(low_type)


def local(
    inputs,
    out_grad,
    attn_weights,
    ffn_weights,
    vectors,
    attn_moment,
    ffn_moment,
    vec_first,
    vec_second,
):
    seq_dev, own_len, width = inputs.shape
    n_ctx = lax.axis_size(ctx_axes)
    n_dp = lax.axis_size(dp_axes)
    n_chip = lax.axis_size(chip_axes)
    ctx = lax.axis_index(ctx_axes)
    core = lax.axis_index("core")
    chip = lax.axis_index(chip_axes)
    length = own_len * n_ctx
    mats, attn_rows = attn_weights.shape[:2]
    ffn_rows = ffn_weights.shape[1]
    hidden_units = n_dp * ffn_rows
    n_vec = vectors.shape[0]
    own_heads = HEADS // n_ctx
    own_cols = own_heads * HD
    block_cols = mats * own_cols
    block_rows = n_ctx * attn_rows
    half = block_rows // 2

    (first_pack,) = call(
        pack_kernel,
        [low(n_ctx, own_len + 2 * attn_rows, width)],
        [
            inputs[0],
            attn_weights,
            attn_moment,
            jnp.pad(vectors[None], ((0, 0), (0, 128 - n_vec))),
        ],
        0,
        name="pack",
    )
    first_pack = trade(first_pack, ctx_axes)
    ffn_all = lax.all_gather(ffn_weights.astype(low_type).reshape(2 * ffn_rows, width), dp_axes)
    ffn_all = ffn_all.reshape(n_chip, 2, 2 * ffn_rows, width)
    x_view = ((n_ctx, own_len, width), (0, 0, 0))
    up_view = ((n_chip, 2, ffn_rows, width), (0, 0, 0, 0))
    down_view = ((n_chip, 2, ffn_rows, width), (0, 0, 1, 0))
    tables = rope_tables(length, own_heads)
    first_pack, tables = lax.optimization_barrier((first_pack, tables))
    small = first_pack[:, own_len : own_len + attn_rows]
    moment_cols = first_pack[:, own_len + attn_rows :].astype(wide_type)
    moment_cols = moment_cols[:, :, : 3 * own_cols] + moment_cols[:, :, 3 * own_cols : 6 * own_cols]
    moment_cols = moment_cols.reshape(block_rows, 3 * own_cols)

    attn_block = small[:, :, :block_cols].reshape(block_rows, block_cols)
    vec_block = small[:, 0, block_cols : block_cols + n_vec].reshape(1, n_ctx * n_vec)
    vec_block = jnp.pad(vec_block, ((0, 0), (0, width - n_ctx * n_vec)))
    pack = jnp.concatenate(
        [
            jnp.concatenate([attn_block[:half], attn_block[half:]], axis=1),
            vec_block,
        ],
        axis=0,
    )
    out_moment = jnp.stack(split_low(attn_moment[3])).reshape(2, attn_rows, n_chip, 2, -1)
    out_moment = out_moment.transpose(2, 3, 0, 1, 4).reshape(n_chip, 2, width)
    out_moment = jnp.pad(out_moment, ((0, 0), (0, 5), (0, 0)))
    pack = jnp.broadcast_to(pack, (n_chip,) + pack.shape)
    pack = trade(jnp.concatenate([pack, out_moment], axis=1), chip_axes)
    pack, moment_cols = lax.optimization_barrier((pack, moment_cols))
    other_pack = swap(pack)
    w_qkv, dy_pack = call(
        unpack_kernel,
        [low(n_chip, 2, block_rows, 3 * own_cols), low(n_ctx, own_len + 32, width)],
        [pack, other_pack, out_grad[0]],
        0,
        flags=[core],
        name="unpack",
    )
    w_qkv = w_qkv.reshape(width, 3 * own_cols)
    dy_pack = trade(dy_pack, ctx_axes)

    vec_rows = [part[:, half, : n_ctx * n_vec] for part in (pack, other_pack)]
    vec_wide = pair(*vec_rows).transpose(1, 0, 2).reshape(-1).astype(wide_type)
    pieces = [vec_wide[index * width : (index + 1) * width] for index in range(9)]
    gain_one, bias_one, gain_two, bias_two, bias_q, bias_k, bias_v, bias_o, bias_down = pieces
    bias_qkv = jnp.concatenate(
        [
            lax.dynamic_slice(piece, (ctx * own_cols,), (own_cols,))
            for piece in (bias_q, bias_k, bias_v)
        ]
    )
    bias_up = lax.dynamic_index_in_dim(
        vec_wide[9 * width :].reshape(n_chip, 2, n_ctx, ffn_rows), ctx, axis=2, keepdims=False
    )
    bias_up = bias_up.transpose(1, 0, 2).reshape(2, n_chip * ffn_rows, 1)
    steps = n_ctx // 2

    def row_block(cols):
        return (length // steps, cols), lambda step: (step, 0)

    x_rows = (n_ctx // steps, own_len, width), lambda step: (step, 0, 0)
    first_in, qkv = call_rows(
        qkv_kernel,
        [low(length, width), low(length, 3 * own_cols)],
        [first_pack, *tables, gain_one[None], bias_one[None], w_qkv, bias_qkv[None]],
        [x_rows, *[row_block(own_cols)] * 3, *[None] * 4, row_block(width), row_block(3 * own_cols)],
        6 * own_cols * length * width,
        steps,
        "qkv",
    )

    second_in, hidden, slope = call(
        ffn_forward_kernel,
        [low(length, width), low(2, hidden_units // 2, length), wide(2, hidden_units // 2, length)],
        [first_pack, gain_two[None], bias_two[None], ffn_all, bias_up],
        2 * hidden_units * length * width,
        views={0: x_view, 3: up_view},
        name="forward",
    )
    dy_pack, qkv, hidden = lax.optimization_barrier((dy_pack, qkv, hidden))
    dy_low, grad_up, kept, given, grad_b_up, w_out, mixed_grad = call(
        ffn_backward_kernel,
        [
            low(length, width),
            low(2, hidden_units // 2, length),
            low(n_chip, 2 * ffn_rows, width),
            low(n_chip, 2 * ffn_rows, width),
            wide(2, 8, n_chip * ffn_rows),
            low(own_cols, width),
            low(own_cols, length),
        ],
        [dy_pack, ffn_all, slope, second_in, hidden],
        (6 * hidden_units + 2 * own_cols) * length * width,
        scratch=[
            pltpu.VMEM((length, width), low_type),
            pltpu.VMEM((n_chip, 2, ffn_rows, width), low_type),
            pltpu.VMEM((2, hidden_units // 2, length), wide_type),
            pltpu.VMEM((length, width), low_type),
            pltpu.VMEM((2, hidden_units // 2, length), low_type),
            pltpu.VMEM((n_ctx, 16, width), low_type),
            pltpu.SemaphoreType.DMA((14,)),
        ],
        flags=[core],
        far=range(5),
        far_out=(0,),
        name="backward",
    )
    ffn_part = (kept.astype(wide_type) + swap(given).astype(wide_type)).astype(low_type)
    ffn_part, mixed_grad = lax.optimization_barrier((ffn_part, mixed_grad))
    out_moment = dy_pack[:, own_len + 16 : own_len + 18].reshape(n_ctx, 2, 2, attn_rows, -1).astype(wide_type).sum(axis=2)
    out_moment = out_moment.transpose(3, 1, 0, 2).reshape(block_rows, own_cols)
    moment_block = jnp.concatenate([moment_cols, out_moment], axis=1)
    ffn_parts = trade(ffn_part, chip_axes)

    mixed, grad_qkv, kept, given = call(
        attention_kernel,
        [
            low(own_cols, length),
            low(length, 3 * own_cols),
            low(n_chip, block_rows, block_cols),
            low(n_chip, block_rows, block_cols),
        ],
        [qkv, mixed_grad, *tables, first_in, dy_low],
        14 * own_cols * length * length + 8 * own_cols * length * width,
        scratch=[
            pltpu.VMEM((own_heads, length, HD), wide_type),
            pltpu.VMEM((own_heads, length, HD), wide_type),
            pltpu.VMEM((width, block_cols), low_type),
            pltpu.VMEM((length, width), low_type),
            pltpu.VMEM((length, width), low_type),
            pltpu.SemaphoreType.DMA((2,)),
        ],
        flags=[core],
        far=(5, 6),
        name="attention",
    )
    grad_block = (kept.astype(wide_type) + swap(given).astype(wide_type)).astype(low_type)
    lane_block = (own_cols, length // steps), lambda step: (0, step)
    unit_block = (2, hidden_units // 2, length // steps), lambda step: (0, 0, step)
    (branch,) = call_rows(
        branch_kernel,
        [wide(length, width)],
        [hidden, mixed, ffn_all, w_out],
        [unit_block, lane_block, (down_view[0], lambda step: down_view[1]), None, row_block(width)],
        2 * (own_cols + hidden_units) * length * width,
        steps,
        "branch",
    )
    grad_block, ffn_parts, branch = lax.optimization_barrier((grad_block, ffn_parts, branch))
    ffn_grad = jnp.sum(ffn_parts.astype(wide_type), axis=0).reshape(2, ffn_rows, width)
    grad_parts = trade(grad_block, chip_axes)
    branch = lax.psum_scatter(branch, ctx_axes, scatter_dimension=0, tiled=True)
    grad_block = jnp.sum(grad_parts.astype(wide_type), axis=0)

    own, ffn_moment_new = call(
        owners_kernel,
        [low(n_chip, ffn_rows, width), wide(2, ffn_rows, width)],
        [ffn_moment, ffn_grad, moment_block, grad_block],
        0,
        name="owners",
    )
    own, grad_qkv = lax.optimization_barrier((own, grad_qkv))
    own = trade(own, chip_axes)
    grad_normed, vec_sums = call_rows(
        normal_kernel,
        [low(length, width), wide(4, width)],
        [grad_qkv, grad_up, first_pack, w_qkv, ffn_all, gain_one[None], gain_two[None]],
        [row_block(3 * own_cols), unit_block, x_rows, None, (up_view[0], lambda step: up_view[1])]
        + [None, None, row_block(width), None],
        2 * (3 * own_cols + hidden_units) * length * width,
        steps,
        "normal",
    )
    own, grad_normed, vec_sums = lax.optimization_barrier((own, grad_normed, vec_sums))
    own_block = own[:, :attn_rows].reshape(n_chip, attn_rows, n_ctx, own_cols).transpose(0, 2, 1, 3)
    own_block = own_block.reshape(width // 2, own_cols)
    own = own.reshape(n_chip * ffn_rows, width)
    owns_ffn = (chip == ffn_owners[0]) | (chip == ffn_owners[1])
    (gram,) = call(
        gram_kernel,
        [low(n_ctx, width // 2, own_cols)],
        [own, swap(own)],
        2 * own.shape[0] * width * width,
        flags=[core],
        name="gram",
    )
    gram = collect(gram, ctx_axes).astype(low_type)
    shard = jnp.where(owns_ffn, gram, own_block)

    own_x = inputs[0].astype(wide_type)
    own_dy = out_grad[0].astype(wide_type)
    bias_sums = jnp.sum(grad_qkv.astype(wide_type), axis=0)
    placed = [
        lax.dynamic_update_slice(
            jnp.zeros((width,), wide_type),
            bias_sums[index * own_cols : (index + 1) * own_cols],
            (ctx * own_cols,),
        )
        for index in range(3)
    ]
    grad_b_up = grad_b_up[:, 0].reshape(2, n_chip, ffn_rows).transpose(1, 0, 2)
    placed_up = lax.dynamic_update_slice(
        jnp.zeros((n_dp, n_ctx, ffn_rows), wide_type),
        grad_b_up.reshape(n_dp, 1, ffn_rows),
        (0, ctx, 0),
    ).reshape(-1)
    grad_bias_out = jnp.sum(own_dy, axis=0)
    vec_part = jnp.concatenate([vec_sums.reshape(-1), *placed, grad_bias_out, grad_bias_out, placed_up])
    vec_part = vec_part.reshape(n_dp, n_ctx, n_vec).transpose(1, 0, 2)
    vec_part = jnp.concatenate(split_low(vec_part), axis=2).reshape(n_ctx, -1)
    n_sent = vec_part.shape[1]
    vec_part = jnp.pad(vec_part, ((0, 0), (0, 8 * width - n_sent))).reshape(n_ctx, -1, own_cols)
    cols_send = jnp.concatenate(split_low(grad_block[:, : 3 * own_cols]), axis=1)
    cols_send = cols_send.reshape(n_ctx, attn_rows, 6 * own_cols)
    out_part = jnp.stack(split_low(grad_block[:, 3 * own_cols :]), axis=1)
    out_part = out_part.reshape(-1, 2, 2, n_ctx, attn_rows).transpose(3, 4, 2, 1, 0)
    out_part = out_part.reshape(n_ctx, attn_rows, 2 * own_cols)
    grad_send = jnp.concatenate([cols_send, out_part], axis=2).reshape(n_ctx, -1, own_cols)
    small_send = jnp.concatenate([vec_part, grad_send], axis=1)
    out_pack = grad_normed.reshape(n_ctx, own_len, width)
    out_pack, small_send, shard = lax.optimization_barrier((out_pack, small_send, shard))
    shard = jnp.broadcast_to(shard, (n_ctx,) + shard.shape)
    shard = trade(jnp.concatenate([shard, small_send], axis=1), ctx_axes)
    out_pack, shard = lax.optimization_barrier((out_pack, shard))
    other = swap(shard)
    out_pack = trade(out_pack, ctx_axes)

    (current,) = call(
        newton_schulz_kernel,
        [low(*own.shape)],
        [shard, other, own],
        20 * width * width * width,
        scratch=[
            pltpu.VMEM((width, width), wide_type),
            pltpu.VMEM((width, width), low_type),
            pltpu.VMEM((width, width), low_type),
            pltpu.VMEM((width, width), low_type),
            pltpu.VMEM(own.shape, wide_type),
        ],
        flags=[owns_ffn, core, ctx, chip == attn_owners[3]],
        name="newton_schulz",
    )
    small_sent, current = lax.optimization_barrier((shard[:, width // 2 :], current))
    out_sum = small_sent[:, : 8 * n_ctx].astype(wide_type).sum(axis=0)
    vec_sum = out_sum.reshape(-1)[:n_sent].reshape(n_chip, 2, 2, n_vec).sum(axis=2)
    vec_kept = lax.dynamic_index_in_dim(vec_sum, core, axis=1, keepdims=False)
    vec_given = lax.dynamic_index_in_dim(vec_sum, 1 - core, axis=1, keepdims=False)
    attn_grad = small_sent[:, 8 * n_ctx :].reshape(n_ctx, attn_rows, width).astype(wide_type)
    cols_grad = attn_grad[:, :, : 3 * own_cols] + attn_grad[:, :, 3 * own_cols : 6 * own_cols]
    cols_grad = cols_grad.reshape(n_ctx, attn_rows, 3, own_cols).transpose(2, 1, 0, 3)
    out_part = attn_grad[:, :, 6 * own_cols :].reshape(n_chip, attn_rows, 2, 2, -1).sum(axis=3)
    out_part = out_part.transpose(2, 0, 1, 3)
    out_kept = lax.dynamic_index_in_dim(out_part, core, axis=0, keepdims=False)
    out_given = lax.dynamic_index_in_dim(out_part, 1 - core, axis=0, keepdims=False)
    both = jnp.concatenate([vec_given, out_given.reshape(n_chip, -1)], axis=1)
    both = swap(both)
    vec_sum = vec_kept + both[:, :n_vec]
    out_part = pair(out_kept, both[:, n_vec:].reshape(out_given.shape)).transpose(1, 2, 0, 3)
    out_part = out_part.reshape(n_chip, attn_rows, own_cols)
    vec_row = jnp.concatenate(split_low(vec_sum), axis=1)
    vec_row = jnp.pad(vec_row[:, None], ((0, 0), (0, attn_rows - 1), (0, width - 2 * own_cols - 2 * n_vec)))
    last_rows = jnp.concatenate([*split_low(out_part), vec_row], axis=2)
    back = jnp.concatenate([current.reshape(n_chip, ffn_rows, width), last_rows], axis=1)
    back, out_pack = lax.optimization_barrier((back, out_pack))
    back = trade(back, chip_axes)
    grad_normed = jnp.sum(out_pack.astype(wide_type), axis=0)
    own_mean = jnp.mean(own_x, axis=-1, keepdims=True)
    own_centered = own_x - own_mean
    own_var = jnp.mean(own_centered * own_centered, axis=-1, keepdims=True)
    own_std = lax.rsqrt(own_var + norm_epsilon)
    own_normed = own_centered * own_std
    grad_center = (
        grad_normed
        - jnp.mean(grad_normed, axis=-1, keepdims=True)
        - own_normed * jnp.mean(grad_normed * own_normed, axis=-1, keepdims=True)
    )
    input_grad = (own_dy + own_std * grad_center)[None]
    back, branch = lax.optimization_barrier((back, branch))
    back = back.astype(wide_type)
    outputs = (own_x + branch + bias_o + bias_down).astype(low_type)[None]
    ortho_ffn = jnp.stack([back[owner, :ffn_rows] for owner in ffn_owners])
    ortho_attn = jnp.stack([back[owner, :attn_rows] for owner in attn_owners])
    last_rows = back[:, ffn_rows:]
    vec_grad = last_rows[:, 0, 2 * own_cols : 2 * own_cols + 2 * n_vec].reshape(n_chip, 2, n_vec)
    vec_grad = vec_grad.sum(axis=(0, 1))
    out_part = last_rows[:, :, :own_cols] + last_rows[:, :, own_cols : 2 * own_cols]
    out_part = out_part.transpose(1, 0, 2).reshape(1, attn_rows, width)
    attn_grad = jnp.concatenate([cols_grad.reshape(3, attn_rows, width), out_part], axis=0)
    attn_moment_new = momentum_decay * attn_moment + attn_grad
    attn_steps = jnp.array([1.0, 1.0, 1.0, 2.0], wide_type)
    ffn_steps = jnp.array([math.sqrt(FF / D), 2.0], wide_type)
    attn_new = (
        attn_weights * (1.0 - learn_rate * weight_decay)
        - learn_rate * attn_steps[:, None, None] * ortho_attn
    )
    ffn_new = (
        ffn_weights * (1.0 - learn_rate * weight_decay)
        - learn_rate * ffn_steps[:, None, None] * ortho_ffn
    )
    vec_first_new = beta_first * vec_first + (1.0 - beta_first) * vec_grad
    vec_second_new = beta_second * vec_second + (1.0 - beta_second) * vec_grad * vec_grad
    first_hat = vec_first_new / (1.0 - beta_first**STEP)
    second_hat = vec_second_new / (1.0 - beta_second**STEP)
    vec_new = vectors - vector_rate * first_hat / (jnp.sqrt(second_hat) + adam_epsilon)
    return (
        outputs,
        input_grad,
        attn_grad,
        ffn_grad,
        vec_grad,
        attn_moment_new,
        ffn_moment_new,
        attn_new,
        ffn_new,
        vec_first_new,
        vec_second_new,
        vec_new,
    )


def solution(mesh):
    names = dp_axes + ctx_axes
    fine = Mesh(mesh.devices.reshape(2, 4, 2, 2, 4), names)
    in_specs = (
        P(dp_axes, ctx_axes, None),
        P(dp_axes, ctx_axes, None),
        P(None, dp_axes + ctx_axes, None),
        P(None, dp_axes + ctx_axes, None),
        P(dp_axes + ctx_axes),
        P(None, dp_axes + ctx_axes, None),
        P(None, dp_axes + ctx_axes, None),
        P(dp_axes + ctx_axes),
        P(dp_axes + ctx_axes),
    )
    out_specs = (
        P(dp_axes, ctx_axes, None),
        P(dp_axes, ctx_axes, None),
        P(None, dp_axes + ctx_axes, None),
        P(None, dp_axes + ctx_axes, None),
        P(dp_axes + ctx_axes),
        P(None, dp_axes + ctx_axes, None),
        P(None, dp_axes + ctx_axes, None),
        P(None, dp_axes + ctx_axes, None),
        P(None, dp_axes + ctx_axes, None),
        P(dp_axes + ctx_axes),
        P(dp_axes + ctx_axes),
        P(dp_axes + ctx_axes),
    )
    return jax.shard_map(local, mesh=fine, in_specs=in_specs, out_specs=out_specs, check_vma=False)
```

```python
import math

import jax
import jax.numpy as jnp
from jax import lax
from jax.experimental import pallas as pl
from jax.experimental.pallas import tpu as pltpu
from jax.sharding import Mesh
from jax.sharding import PartitionSpec as P

D = 1024
FF = 4096
HEADS = 16
HD = 64
ROT = 16
ITERS = 3
STEP = 10


norm_epsilon = 1e-05
quintic_one = 3.4445
quintic_two = -4.775
quintic_three = 2.0315
momentum_decay = 0.95
learn_rate = 0.4
weight_decay = 0.01
beta_first = 0.9
beta_second = 0.95
vector_rate = 0.05
adam_epsilon = 1e-08

low_type = jnp.bfloat16
wide_type = jnp.float32
dp_axes = ("z_lo", "x", "core")
ctx_axes = ("z_hi", "y")
chip_axes = ("z_lo", "x")
ffn_owners = (0, 6)
attn_owners = (1, 3, 5, 7)


def trade(blocks, axes):
    return lax.all_to_all(blocks, axes, split_axis=0, concat_axis=0, tiled=True)


def spread(block, axes):
    return trade(jnp.broadcast_to(block, (lax.axis_size(axes),) + block.shape), axes)


def collect(partials, axes):
    return jnp.sum(trade(partials.astype(low_type), axes).astype(wide_type), axis=0)


def swap(block):
    return lax.ppermute(block, "core", [(0, 1), (1, 0)])


def halve(pairs):
    core = lax.axis_index("core")
    kept = lax.dynamic_index_in_dim(pairs, core, axis=0, keepdims=False)
    given = lax.dynamic_index_in_dim(pairs, 1 - core, axis=0, keepdims=False)
    return kept.astype(wide_type) + swap(given).astype(wide_type)


def pair(mine, other):
    first = lax.axis_index("core") == 0
    return jnp.stack([jnp.where(first, mine, other), jnp.where(first, other, mine)])


def split_low(wide):
    high = lax.reduce_precision(wide, 8, 7)
    return high.astype(low_type), (wide - high).astype(low_type)


def dot(left, right):
    return jnp.dot(left, right, preferred_element_type=wide_type)


def dot_nt(left, right):
    return lax.dot_general(
        left, right, (((1,), (1,)), ((), ())), preferred_element_type=wide_type
    )


def dot_tn(left, right):
    return lax.dot_general(
        left, right, (((0,), (0,)), ((), ())), preferred_element_type=wide_type
    )


def rope_tables(length, heads):
    lane = lax.rem(jnp.arange(heads * HD, dtype=jnp.int32), HD)
    half_rot = ROT // 2
    inv_freq = 10000.0 ** (-(lax.rem(lane, half_rot).astype(wide_type) * 2.0) / ROT)
    angles = jnp.arange(length, dtype=jnp.int32).astype(wide_type)[:, None] * inv_freq[None, :]
    keep = jnp.where(lane < ROT, jnp.cos(angles), 1.0)
    sines = jnp.sin(angles)
    ahead = jnp.where(lane < half_rot, -sines, 0.0)
    behind = jnp.where((lane >= half_rot) & (lane < ROT), sines, 0.0)
    return keep, ahead, behind


def turned(rows, tables):
    half_rot = ROT // 2
    cols = rows.shape[1]
    ahead = pltpu.roll(rows, cols - half_rot, 1)
    behind = pltpu.roll(rows, half_rot, 1)
    return ahead * tables[1] + behind * tables[2]


def attention_kernel(
    flags_ref, qkv_ref, mixed_grad_ref, keep_ref, ahead_ref, behind_ref, first_far, dy_far, mixed_ref, grad_ref, g_kept_ref,
    g_given_ref, k_sum, v_sum, g_all, first_ref, dy_ref, sems
):
    length, cols = keep_ref.shape
    heads = cols // HD
    scale = HD ** (-0.5)
    tables = (keep_ref[...], ahead_ref[...], behind_ref[...])
    first_copy = pltpu.make_async_copy(first_far, first_ref, sems.at[0])
    dy_copy = pltpu.make_async_copy(dy_far, dy_ref, sems.at[1])
    first_copy.start()
    dy_copy.start()
    q_rot = qkv_ref[:, :cols]
    k_rot = qkv_ref[:, cols : 2 * cols]
    v_low = qkv_ref[:, 2 * cols :]
    k_sum[...] = jnp.zeros_like(k_sum)
    v_sum[...] = jnp.zeros_like(v_sum)
    block = 256
    for start in range(0, length, block):
        stop = start + block
        q_grads = []
        for head in range(heads):
            lanes = slice(head*HD, (head+1)*HD)
            q_now, k_now, v_now = q_rot[start:stop, lanes], k_rot[:stop, lanes], v_low[:stop, lanes]
            grad_t = mixed_grad_ref[lanes, start:stop]
            raw = dot_nt(k_now, q_now) * scale
            key_pos = lax.broadcasted_iota(jnp.int32, (stop, block), 0)
            query_pos = lax.broadcasted_iota(jnp.int32, (stop, block), 1) + start
            scores = jnp.where(key_pos <= query_pos, raw, -1e30)
            expo = jnp.exp(scores - jnp.max(scores, axis=0, keepdims=True))
            probs = expo * (1.0 / jnp.sum(expo, axis=0, keepdims=True))
            probs_low = probs.astype(low_type)
            mixed_ref[lanes, start:stop] = dot_tn(v_now, probs_low).astype(low_type)
            grad_probs = dot(v_now, grad_t)
            inner = jnp.sum(probs * grad_probs, axis=0, keepdims=True)
            grad_raw = (probs * (grad_probs - inner) * scale).astype(low_type)
            q_grads.append(dot_tn(k_now, grad_raw))
            k_sum[head, :stop, :] += dot(grad_raw, q_now)
            v_sum[head, :stop, :] += dot_nt(probs_low, grad_t)
        grad_q = jnp.concatenate(q_grads, axis=0).T
        part = tuple(table[start:stop] for table in tables)
        grad_ref[start:stop, :cols] = (grad_q * part[0] - turned(grad_q, part)).astype(low_type)
    grad_k = jnp.concatenate([k_sum[head] for head in range(heads)], axis=1)
    grad_v = jnp.concatenate([v_sum[head] for head in range(heads)], axis=1)
    grad_ref[:, cols:2*cols] = (grad_k * tables[0] - turned(grad_k, tables)).astype(low_type)
    grad_ref[:, 2*cols:] = grad_v.astype(low_type)
    first_copy.wait()
    dy_copy.wait()
    for start in range(0, first_ref.shape[1], block):
        g_all[start : start + block, : 3 * cols] = dot_tn(
            first_ref[:, start : start + block], grad_ref[...]
        ).astype(low_type)
        g_all[start : start + block, 3 * cols :] = dot(
            mixed_ref[...], dy_ref[:, start : start + block]
        ).T.astype(low_type)
    chips, part = g_kept_ref.shape[:2]
    core = flags_ref[0]
    for chip in range(chips):
        for place, out_ref in ((core, g_kept_ref), (1 - core, g_given_ref)):
            out_ref[chip] = g_all[pl.ds(pl.multiple_of((2 * chip + place) * part, part), part)]


def vmem_specs(count):
    return [pl.BlockSpec(memory_space=pltpu.VMEM)] * count


def call(kernel, outs, args, flops, scratch=(), flags=None, name=None, views={}, far=(), far_out=()):
    specs, size = [], 0
    for index, each in enumerate(args):
        block, place = views.get(index, (each.shape, (0,) * each.ndim))
        if index in far:
            specs.append(pl.BlockSpec(memory_space=pl.ANY))
        else:
            specs.append(pl.BlockSpec(block, lambda step, place=place: place))
        size += math.prod(block) * each.dtype.itemsize
    size += sum(math.prod(each.shape) * each.dtype.itemsize for each in outs)
    args = list(args)
    if flags is not None:
        specs = [pl.BlockSpec(memory_space=pltpu.SMEM)] + specs
        args = [jnp.stack([jnp.asarray(flag, jnp.int32) for flag in flags])] + args
    return pl.pallas_call(
        kernel,
        grid=(1,),
        out_shape=tuple(outs),
        in_specs=specs,
        out_specs=tuple(
            pl.BlockSpec(memory_space=pl.ANY)
            if index in far_out
            else pl.BlockSpec(each.shape, lambda step, rank=len(each.shape): (0,) * rank)
            for index, each in enumerate(outs)
        ),
        scratch_shapes=list(scratch),
        compiler_params=pltpu.CompilerParams(vmem_limit_bytes=60 * 1024 * 1024),
        cost_estimate=pl.CostEstimate(flops=flops, bytes_accessed=size, transcendentals=0),
        name=name,
    )(*args)


def wide(*shape):
    return jax.ShapeDtypeStruct(shape, wide_type)


def low(*shape):
    return jax.ShapeDtypeStruct(shape, low_type)


def normalized(rows):
    rows = rows.astype(wide_type)
    centered = rows - jnp.mean(rows, axis=-1, keepdims=True)
    variance = jnp.mean(centered * centered, axis=-1, keepdims=True)
    return centered * lax.rsqrt(variance + norm_epsilon)


def pack_kernel(x_ref, weights_ref, moment_ref, vec_ref, out_ref):
    tokens = x_ref.shape[0]
    cols = weights_ref.shape[2] // out_ref.shape[0]
    for target in range(out_ref.shape[0]):
        lanes = slice(target * cols, (target + 1) * cols)
        out_ref[target, :tokens] = x_ref[...]
        vec = jnp.broadcast_to(vec_ref[...], (weights_ref.shape[1], vec_ref.shape[1]))
        weights = [weights_ref[index, :, lanes] for index in range(4)]
        blank = jnp.zeros((weights_ref.shape[1], 4 * cols - vec_ref.shape[1]), wide_type)
        moments = [moment_ref[index, :, lanes] for index in range(3)]
        highs = [moment.astype(low_type).astype(wide_type) for moment in moments]
        lows = [moment - high for moment, high in zip(moments, highs)]
        rest = jnp.zeros((weights_ref.shape[1], 2 * cols), wide_type)
        upper = jnp.concatenate([*weights, vec, blank], axis=1)
        lower = jnp.concatenate([*highs, *lows, rest], axis=1)
        out_ref[target, tokens:] = jnp.concatenate([upper, lower], axis=0).astype(low_type)


def owners_kernel(ffn_moment_ref, ffn_grad_ref, moment_ref, grad_ref, out_ref, ffn_new_ref):
    for index, owner in enumerate(ffn_owners):
        rows = momentum_decay * ffn_moment_ref[index] + ffn_grad_ref[index]
        ffn_new_ref[index] = rows
        out_ref[owner] = rows.astype(low_type)
    block = momentum_decay * moment_ref[...] + grad_ref[...]
    cols, rows = block.shape[1] // 4, 8
    groups = block.shape[0] // rows
    blank = jnp.zeros((out_ref.shape[1] - rows, out_ref.shape[2]), wide_type)
    for index, owner in enumerate(attn_owners):
        lanes = slice(index * cols, (index + 1) * cols)
        parts = [block[rows * group : rows * (group + 1), lanes] for group in range(groups)]
        filled = jnp.concatenate([jnp.concatenate(parts, axis=1), blank], axis=0)
        out_ref[owner] = filled.astype(low_type)
    for owner in range(out_ref.shape[0]):
        if owner not in ffn_owners + attn_owners:
            out_ref[owner] = jnp.zeros(out_ref.shape[1:], low_type)


def unpack_kernel(flags_ref, mine_ref, other_ref, dy_ref, qkv_ref, out_ref):
    half, tokens, cols = 32, dy_ref.shape[0], out_ref.shape[2] // 8
    first = flags_ref[0] == 0
    mine, other = mine_ref[:, :half], other_ref[:, :half]
    for core, part in enumerate((jnp.where(first, mine, other), jnp.where(first, other, mine))):
        for upper in range(2):
            lanes = part[:, :, upper * 4 * cols : (upper + 1) * 4 * cols]
            qkv_ref[:, core, upper * half : (upper + 1) * half] = lanes[:, :, : 3 * cols]
            for group in range(2):
                place = (4 * core + 2 * upper + group) * cols
                out_ref[:, tokens : tokens + 16, place : place + cols] = lanes[
                    :, 16 * group : 16 * (group + 1), 3 * cols :
                ]
    rows = []
    for ref in (mine_ref, other_ref):
        last = ref[:, half:].astype(wide_type)
        rows.append(jnp.where(first, last[:, 1:2], last[:, 2:3]))
    blank = jnp.zeros((out_ref.shape[0], 14, out_ref.shape[2]), wide_type)
    pair_rows = [jnp.where(first, rows[0], rows[1]), jnp.where(first, rows[1], rows[0])]
    out_ref[:, tokens + 16 :] = jnp.concatenate([*pair_rows, blank], axis=1).astype(low_type)
    for target in range(out_ref.shape[0]):
        out_ref[target, :tokens] = dy_ref[...]


def qkv_kernel(
    x_ref, keep_ref, ahead_ref, behind_ref, gain_ref, shift_ref, w_ref, bias_ref, first_ref, out_ref
):
    cols = keep_ref.shape[1]
    tables = (keep_ref[...], ahead_ref[...], behind_ref[...])
    normed = normalized(x_ref[...].reshape(first_ref.shape))
    first = (normed * gain_ref[...] + shift_ref[...]).astype(low_type)
    first_ref[...] = first
    rows = dot(first, w_ref[...]) + bias_ref[...]
    for index in range(2):
        part = rows[:, index * cols : (index + 1) * cols]
        out_ref[:, index * cols : (index + 1) * cols] = (
            part * tables[0] + turned(part, tables)
        ).astype(low_type)
    out_ref[:, 2 * cols :] = rows[:, 2 * cols :].astype(low_type)


def ffn_forward_kernel(x_ref, gain_ref, shift_ref, up_ref, bias_ref, second_ref, hidden_ref, slope_ref):
    sources, tokens, width = x_ref.shape
    for source in range(sources):
        second_ref[source * tokens : (source + 1) * tokens] = (
            normalized(x_ref[source]) * gain_ref[...] + shift_ref[...]
        ).astype(low_type)
    for index in range(2):
        pre = dot_nt(up_ref[:, index].reshape(-1, width), second_ref[...]) + bias_ref[index]
        chance = 0.5 * (1.0 + lax.erf(pre * math.sqrt(0.5)))
        density = jnp.exp(-0.5 * pre * pre) * (1.0 / math.sqrt(2.0 * math.pi))
        hidden_ref[index] = (pre * chance).astype(low_type)
        slope_ref[index] = chance + pre * density


def ffn_backward_kernel(
    flags_ref, pack_ref, rows_ref, slope_ref, second_ref, hidden_ref, dy_ref, grad_up_ref, kept_ref,
    given_ref, g_bias_ref, w_out_ref, mixed_grad_ref, dy, down, slope, second, hidden, out_rows, sems
):
    chips, units, width = kept_ref.shape
    units = units // 2
    sources, tokens = pack_ref.shape[0], pack_ref.shape[1] - 32
    copies = []

    def fetch(source, target):
        copy = pltpu.make_async_copy(source, target, sems.at[len(copies)])
        copy.start()
        copies.append(copy)
        return copy

    parts = []
    for source in range(sources):
        parts.append(
            fetch(pack_ref.at[source, pl.ds(0, tokens)], dy.at[pl.ds(source * tokens, tokens)])
        )
    parts.append(fetch(rows_ref.at[:, :, pl.ds(units, units)], down))
    slope_copy = fetch(slope_ref, slope)
    second_copy = fetch(second_ref, second)
    hidden_copy = fetch(hidden_ref, hidden)
    out_copy = fetch(pack_ref.at[:, pl.ds(tokens, 16)], out_rows)
    for part in parts:
        part.wait()
    back_copy = fetch(dy, dy_ref)
    ones = jnp.ones((8, dy.shape[0]), low_type)
    for index in range(2):
        grad_hidden = dot_nt(down[:, index].reshape(-1, width), dy[...])
        if index == 0:
            slope_copy.wait()
        grad_up = (grad_hidden * slope[index]).astype(low_type)
        grad_up_ref[index] = grad_up
        g_bias_ref[index] = dot_nt(ones, grad_up)
        if index == 0:
            second_copy.wait()
        g_up = dot(grad_up, second[...]).astype(low_type).reshape(chips, units, width)
        if index == 0:
            hidden_copy.wait()
        g_down = dot(hidden[index], dy[...]).astype(low_type).reshape(chips, units, width)

        @pl.when(flags_ref[0] == index)
        def _():
            kept_ref[:, :units] = g_up
            kept_ref[:, units:] = g_down

        @pl.when(flags_ref[0] != index)
        def _():
            given_ref[:, :units] = g_up
            given_ref[:, units:] = g_down

    out_copy.wait()
    cols = width // sources
    for source in range(sources):
        for group in range(8):
            w_out_ref[16 * group : 16 * (group + 1), source * cols : (source + 1) * cols] = out_rows[
                source, :, group * cols : (group + 1) * cols
            ]
    mixed_grad_ref[...] = dot_nt(w_out_ref[...], dy[...]).astype(low_type)
    back_copy.wait()


def normal_kernel(
    grad_ref, grad_up_ref, x_ref, w_ref, rows_ref, gain_one_ref, gain_two_ref, out_ref, sums_ref
):
    first = dot_nt(grad_ref[...], w_ref[...])
    second = 0.0
    for index in range(2):
        up = rows_ref[:, index].reshape(-1, first.shape[1])
        second = second + dot_tn(grad_up_ref[index], up)
    normed = normalized(x_ref[...].reshape(first.shape))
    out_ref[...] = (first * gain_one_ref[...] + second * gain_two_ref[...]).astype(low_type)
    terms = (first * normed, first, second * normed, second)
    sums = jnp.concatenate([jnp.sum(term, axis=0, keepdims=True) for term in terms], axis=0)

    @pl.when(pl.program_id(0) == 0)
    def _():
        sums_ref[...] = jnp.zeros_like(sums_ref)

    sums_ref[...] += sums


def branch_kernel(hidden_ref, mixed_ref, rows_ref, w_out_ref, out_ref, mark_ref):
    total = dot_tn(mixed_ref[...], w_out_ref[...])
    for index in range(2):
        down = rows_ref[:, index].reshape(-1, total.shape[1])
        total = total + dot_tn(hidden_ref[index], down)
    out_ref[...] = total
    mark_ref[...] = total[:8, :128]


def gram_kernel(flags_ref, own_ref, other_ref, out_ref):
    half, cols = out_ref.shape[1:]
    lanes = pl.ds(pl.multiple_of(flags_ref[0] * half, half), half)
    rows = dot_tn(own_ref[:, lanes], own_ref[...]) + dot_tn(other_ref[:, lanes], other_ref[...])
    for index in range(out_ref.shape[0]):
        out_ref[index] = rows[:, index * cols : (index + 1) * cols].astype(low_type)


def call_rows(kernel, outs, args, blocks, flops, steps, name):
    arrays = list(args) + list(outs)
    specs, size = [], 0
    for each, given in zip(arrays, blocks):
        shape, place = given or (each.shape, lambda step, rank=len(each.shape): (0,) * rank)
        specs.append(pl.BlockSpec(shape, place))
        size += math.prod(shape) * each.dtype.itemsize * (steps if given else 1)
    return pl.pallas_call(
        kernel,
        grid=(steps,),
        out_shape=tuple(outs),
        in_specs=specs[: len(args)],
        out_specs=tuple(specs[len(args) :]),
        compiler_params=pltpu.CompilerParams(vmem_limit_bytes=60 * 1024 * 1024),
        cost_estimate=pl.CostEstimate(flops=flops, bytes_accessed=size, transcendentals=0),
        name=name,
    )(*args)


def newton_schulz_kernel(
    flags_ref, mine_ref, other_ref, rows_ref, out_ref, gram_ref, low_ref, mixer_ref, start_ref, current_ref
):
    width = rows_ref.shape[1]
    half = width // 2
    block = 512
    chips = 8
    attn_rows, units = 8, rows_ref.shape[0] // chips
    core, ctx = flags_ref[1], flags_ref[2]
    cols = mine_ref.shape[2]
    part = half // chips

    @pl.when(flags_ref[0] == 1)
    def _():
        for source in range(mine_ref.shape[0]):
            lanes = slice(source * cols, (source + 1) * cols)
            for place, ref in ((core, mine_ref), (1 - core, other_ref)):
                rows = pl.ds(pl.multiple_of(place * half, half), half)
                gram_ref[rows, lanes] = ref[source, :half].astype(wide_type)
        total = jnp.zeros((1, 1), wide_type)
        for start in range(0, width, 256):
            square = gram_ref[start : start + 256, start : start + 256]
            diagonal = lax.broadcasted_iota(jnp.int32, square.shape, 0) == lax.broadcasted_iota(
                jnp.int32, square.shape, 1
            )
            total = total + jnp.sum(jnp.where(diagonal, square, 0.0), keepdims=True)
        factor = 1.0 / (jnp.sqrt(total) + 1e-07)
        gram_ref[...] = gram_ref[...] * (factor * factor)
        current_ref[...] = rows_ref[...].astype(wide_type) * factor

    @pl.when(flags_ref[0] == 0)
    def _():
        for source in range(mine_ref.shape[0]):
            lanes = slice(source * cols, (source + 1) * cols)
            for chip in range(chips):
                for place, ref in ((core, mine_ref), (1 - core, other_ref)):
                    rows = pl.ds(pl.multiple_of((2 * chip + place) * part, part), part)
                    gram_ref[rows, lanes] = ref[source, chip * part : (chip + 1) * part].astype(wide_type)
        raw = gram_ref[...]
        factor = 1.0 / (jnp.sqrt(jnp.sum(raw * raw, keepdims=True)) + 1e-07)
        start_ref[...] = (raw * factor).astype(low_type)
        blank = jnp.zeros((units - attn_rows, width), wide_type)
        for chip in range(chips):
            place = pl.multiple_of((2 * chip + core) * part + attn_rows * ctx, attn_rows)
            rows = gram_ref[pl.ds(place, attn_rows)] * factor
            current_ref[units * chip : units * (chip + 1)] = jnp.concatenate([rows, blank])

        @pl.when(flags_ref[3] == 1)
        def _():
            row = lax.broadcasted_iota(jnp.int32, current_ref.shape, 0)
            inner = lax.rem(row, units)
            place = (lax.div(row, units) * 2 + core) * part + attn_rows * ctx + inner
            lane = lax.broadcasted_iota(jnp.int32, current_ref.shape, 1)
            current_ref[...] = jnp.where((lane == place) & (inner < attn_rows), 1.0, 0.0)

        for start in range(0, width, 256):
            lanes = slice(start, start + 256)
            gram_ref[lanes] = dot_tn(start_ref[:, lanes], start_ref[...])

    def mix(index, carry):
        rows = pl.ds(pl.multiple_of(index * block, block), block)
        square = dot(low_ref[rows], low_ref[...])
        mixer_ref[rows] = (quintic_two * gram_ref[rows] + quintic_three * square).astype(low_type)
        return carry

    def advance(index, carry):
        rows = pl.ds(pl.multiple_of(index * block, block), block)
        turn = quintic_one * gram_ref[rows] + dot(low_ref[rows], mixer_ref[...])
        gram_ref[rows] = quintic_one * turn + dot(turn.astype(low_type), mixer_ref[...])
        return carry

    def times(rows, matrix_ref):
        return dot(rows.astype(low_type), matrix_ref[...])

    def factor_times(rows):
        return quintic_one * rows + times(rows, mixer_ref)

    for repeat in range(2):
        low_ref[...] = gram_ref[...].astype(low_type)
        lax.fori_loop(0, width // block, mix, 0)
        current_ref[...] = factor_times(current_ref[...])
        if repeat == 0:
            lax.fori_loop(0, width // block, advance, 0)

    def third_gram_times(rows):
        return factor_times(times(factor_times(rows), low_ref))

    current = current_ref[...]
    once = third_gram_times(current)
    twice = third_gram_times(once)
    current_ref[...] = quintic_one * current + quintic_two * once + quintic_three * twice
    out_ref[...] = current_ref[...].astype(low_type)

    @pl.when(flags_ref[3] == 1)
    def _():
        out_ref[...] = dot_nt(out_ref[...], start_ref[...]).astype(low_type)


def local(
    inputs,
    out_grad,
    attn_weights,
    ffn_weights,
    vectors,
    attn_moment,
    ffn_moment,
    vec_first,
    vec_second,
):
    seq_dev, own_len, width = inputs.shape
    n_ctx = lax.axis_size(ctx_axes)
    n_dp = lax.axis_size(dp_axes)
    n_chip = lax.axis_size(chip_axes)
    ctx = lax.axis_index(ctx_axes)
    core = lax.axis_index("core")
    chip = lax.axis_index(chip_axes)
    length = own_len * n_ctx
    mats, attn_rows = attn_weights.shape[:2]
    ffn_rows = ffn_weights.shape[1]
    hidden_units = n_dp * ffn_rows
    n_vec = vectors.shape[0]
    own_heads = HEADS // n_ctx
    own_cols = own_heads * HD
    block_cols = mats * own_cols
    block_rows = n_ctx * attn_rows
    half = block_rows // 2

    (first_pack,) = call(
        pack_kernel,
        [low(n_ctx, own_len + 2 * attn_rows, width)],
        [
            inputs[0],
            attn_weights,
            attn_moment,
            jnp.pad(vectors[None], ((0, 0), (0, 128 - n_vec))),
        ],
        0,
        name="pack",
    )
    first_pack = trade(first_pack, ctx_axes)
    ffn_all = lax.all_gather(ffn_weights.astype(low_type).reshape(2 * ffn_rows, width), dp_axes)
    ffn_all = ffn_all.reshape(n_chip, 2, 2 * ffn_rows, width)
    x_view = ((n_ctx, own_len, width), (0, 0, 0))
    up_view = ((n_chip, 2, ffn_rows, width), (0, 0, 0, 0))
    down_view = ((n_chip, 2, ffn_rows, width), (0, 0, 1, 0))
    tables = rope_tables(length, own_heads)
    first_pack, tables = lax.optimization_barrier((first_pack, tables))
    small = first_pack[:, own_len : own_len + attn_rows]
    moment_cols = first_pack[:, own_len + attn_rows :].astype(wide_type)
    moment_cols = moment_cols[:, :, : 3 * own_cols] + moment_cols[:, :, 3 * own_cols : 6 * own_cols]
    moment_cols = moment_cols.reshape(block_rows, 3 * own_cols)

    attn_block = small[:, :, :block_cols].reshape(block_rows, block_cols)
    vec_block = small[:, 0, block_cols : block_cols + n_vec].reshape(1, n_ctx * n_vec)
    vec_block = jnp.pad(vec_block, ((0, 0), (0, width - n_ctx * n_vec)))
    pack = jnp.concatenate(
        [
            jnp.concatenate([attn_block[:half], attn_block[half:]], axis=1),
            vec_block,
        ],
        axis=0,
    )
    out_moment = jnp.stack(split_low(attn_moment[3])).reshape(2, attn_rows, n_chip, 2, -1)
    out_moment = out_moment.transpose(2, 3, 0, 1, 4).reshape(n_chip, 2, width)
    out_moment = jnp.pad(out_moment, ((0, 0), (0, 5), (0, 0)))
    pack = jnp.broadcast_to(pack, (n_chip,) + pack.shape)
    pack = trade(jnp.concatenate([pack, out_moment], axis=1), chip_axes)
    pack, moment_cols = lax.optimization_barrier((pack, moment_cols))
    other_pack = swap(pack)
    w_qkv, dy_pack = call(
        unpack_kernel,
        [low(n_chip, 2, block_rows, 3 * own_cols), low(n_ctx, own_len + 32, width)],
        [pack, other_pack, out_grad[0]],
        0,
        flags=[core],
        name="unpack",
    )
    w_qkv = w_qkv.reshape(width, 3 * own_cols)
    dy_pack = trade(dy_pack, ctx_axes)

    vec_rows = [part[:, half, : n_ctx * n_vec] for part in (pack, other_pack)]
    vec_wide = pair(*vec_rows).transpose(1, 0, 2).reshape(-1).astype(wide_type)
    pieces = [vec_wide[index * width : (index + 1) * width] for index in range(9)]
    gain_one, bias_one, gain_two, bias_two, bias_q, bias_k, bias_v, bias_o, bias_down = pieces
    bias_qkv = jnp.concatenate(
        [
            lax.dynamic_slice(piece, (ctx * own_cols,), (own_cols,))
            for piece in (bias_q, bias_k, bias_v)
        ]
    )
    bias_up = lax.dynamic_index_in_dim(
        vec_wide[9 * width :].reshape(n_chip, 2, n_ctx, ffn_rows), ctx, axis=2, keepdims=False
    )
    bias_up = bias_up.transpose(1, 0, 2).reshape(2, n_chip * ffn_rows, 1)
    steps = n_ctx // 2

    def row_block(cols):
        return (length // steps, cols), lambda step: (step, 0)

    x_rows = (n_ctx // steps, own_len, width), lambda step: (step, 0, 0)
    first_in, qkv = call_rows(
        qkv_kernel,
        [low(length, width), low(length, 3 * own_cols)],
        [first_pack, *tables, gain_one[None], bias_one[None], w_qkv, bias_qkv[None]],
        [x_rows, *[row_block(own_cols)] * 3, *[None] * 4, row_block(width), row_block(3 * own_cols)],
        6 * own_cols * length * width,
        steps,
        "qkv",
    )

    second_in, hidden, slope = call(
        ffn_forward_kernel,
        [low(length, width), low(2, hidden_units // 2, length), wide(2, hidden_units // 2, length)],
        [first_pack, gain_two[None], bias_two[None], ffn_all, bias_up],
        2 * hidden_units * length * width,
        views={0: x_view, 3: up_view},
        name="forward",
    )
    dy_pack, qkv, hidden = lax.optimization_barrier((dy_pack, qkv, hidden))
    dy_low, grad_up, kept, given, grad_b_up, w_out, mixed_grad = call(
        ffn_backward_kernel,
        [
            low(length, width),
            low(2, hidden_units // 2, length),
            low(n_chip, 2 * ffn_rows, width),
            low(n_chip, 2 * ffn_rows, width),
            wide(2, 8, n_chip * ffn_rows),
            low(own_cols, width),
            low(own_cols, length),
        ],
        [dy_pack, ffn_all, slope, second_in, hidden],
        (6 * hidden_units + 2 * own_cols) * length * width,
        scratch=[
            pltpu.VMEM((length, width), low_type),
            pltpu.VMEM((n_chip, 2, ffn_rows, width), low_type),
            pltpu.VMEM((2, hidden_units // 2, length), wide_type),
            pltpu.VMEM((length, width), low_type),
            pltpu.VMEM((2, hidden_units // 2, length), low_type),
            pltpu.VMEM((n_ctx, 16, width), low_type),
            pltpu.SemaphoreType.DMA((14,)),
        ],
        flags=[core],
        far=range(5),
        far_out=(0,),
        name="backward",
    )
    ffn_part = (kept.astype(wide_type) + swap(given).astype(wide_type)).astype(low_type)
    ffn_part, mixed_grad = lax.optimization_barrier((ffn_part, mixed_grad))
    out_moment = dy_pack[:, own_len + 16 : own_len + 18].reshape(n_ctx, 2, 2, attn_rows, -1).astype(wide_type).sum(axis=2)
    out_moment = out_moment.transpose(3, 1, 0, 2).reshape(block_rows, own_cols)
    moment_block = jnp.concatenate([moment_cols, out_moment], axis=1)
    ffn_parts = trade(ffn_part, chip_axes)

    mixed, grad_qkv, kept, given = call(
        attention_kernel,
        [
            low(own_cols, length),
            low(length, 3 * own_cols),
            low(n_chip, block_rows, block_cols),
            low(n_chip, block_rows, block_cols),
        ],
        [qkv, mixed_grad, *tables, first_in, dy_low],
        14 * own_cols * length * length + 8 * own_cols * length * width,
        scratch=[
            pltpu.VMEM((own_heads, length, HD), wide_type),
            pltpu.VMEM((own_heads, length, HD), wide_type),
            pltpu.VMEM((width, block_cols), low_type),
            pltpu.VMEM((length, width), low_type),
            pltpu.VMEM((length, width), low_type),
            pltpu.SemaphoreType.DMA((2,)),
        ],
        flags=[core],
        far=(5, 6),
        name="attention",
    )
    grad_block = (kept.astype(wide_type) + swap(given).astype(wide_type)).astype(low_type)
    lane_block = (own_cols, length // steps), lambda step: (0, step)
    unit_block = (2, hidden_units // 2, length // steps), lambda step: (0, 0, step)
    branch, mark = call_rows(
        branch_kernel,
        [wide(length, width), wide(8, 128)],
        [hidden, mixed, ffn_all, w_out],
        [unit_block, lane_block, (down_view[0], lambda step: down_view[1]), None, row_block(width), None],
        2 * (own_cols + hidden_units) * length * width,
        steps,
        "branch",
    )
    grad_block, ffn_parts = lax.optimization_barrier((grad_block, ffn_parts))
    ffn_grad = jnp.sum(ffn_parts.astype(wide_type), axis=0).reshape(2, ffn_rows, width)
    grad_parts = trade(grad_block, chip_axes)
    grad_parts, mark = lax.optimization_barrier((grad_parts, mark))
    branch = lax.psum_scatter(branch, ctx_axes, scatter_dimension=0, tiled=True)
    grad_block = jnp.sum(grad_parts.astype(wide_type), axis=0)

    own, ffn_moment_new = call(
        owners_kernel,
        [low(n_chip, ffn_rows, width), wide(2, ffn_rows, width)],
        [ffn_moment, ffn_grad, moment_block, grad_block],
        0,
        name="owners",
    )
    own, grad_qkv = lax.optimization_barrier((own, grad_qkv))
    own = trade(own, chip_axes)
    grad_normed, vec_sums = call_rows(
        normal_kernel,
        [low(length, width), wide(4, width)],
        [grad_qkv, grad_up, first_pack, w_qkv, ffn_all, gain_one[None], gain_two[None]],
        [row_block(3 * own_cols), unit_block, x_rows, None, (up_view[0], lambda step: up_view[1])]
        + [None, None, row_block(width), None],
        2 * (3 * own_cols + hidden_units) * length * width,
        steps,
        "normal",
    )
    own, grad_normed, vec_sums = lax.optimization_barrier((own, grad_normed, vec_sums))
    own_block = own[:, :attn_rows].reshape(n_chip, attn_rows, n_ctx, own_cols).transpose(0, 2, 1, 3)
    own_block = own_block.reshape(width // 2, own_cols)
    own = own.reshape(n_chip * ffn_rows, width)
    owns_ffn = (chip == ffn_owners[0]) | (chip == ffn_owners[1])
    (gram,) = call(
        gram_kernel,
        [low(n_ctx, width // 2, own_cols)],
        [own, swap(own)],
        2 * own.shape[0] * width * width,
        flags=[core],
        name="gram",
    )
    gram = collect(gram, ctx_axes).astype(low_type)
    shard = jnp.where(owns_ffn, gram, own_block)

    own_x = inputs[0].astype(wide_type)
    own_dy = out_grad[0].astype(wide_type)
    bias_sums = jnp.sum(grad_qkv.astype(wide_type), axis=0)
    placed = [
        lax.dynamic_update_slice(
            jnp.zeros((width,), wide_type),
            bias_sums[index * own_cols : (index + 1) * own_cols],
            (ctx * own_cols,),
        )
        for index in range(3)
    ]
    grad_b_up = grad_b_up[:, 0].reshape(2, n_chip, ffn_rows).transpose(1, 0, 2)
    placed_up = lax.dynamic_update_slice(
        jnp.zeros((n_dp, n_ctx, ffn_rows), wide_type),
        grad_b_up.reshape(n_dp, 1, ffn_rows),
        (0, ctx, 0),
    ).reshape(-1)
    grad_bias_out = jnp.sum(own_dy, axis=0)
    vec_part = jnp.concatenate([vec_sums.reshape(-1), *placed, grad_bias_out, grad_bias_out, placed_up])
    vec_part = vec_part.reshape(n_dp, n_ctx, n_vec).transpose(1, 0, 2)
    vec_part = jnp.concatenate(split_low(vec_part), axis=2).reshape(n_ctx, -1)
    n_sent = vec_part.shape[1]
    vec_part = jnp.pad(vec_part, ((0, 0), (0, 4 * width - n_sent))).reshape(n_ctx, -1, own_cols)
    vec_lines = vec_part.shape[1]
    cols_send = jnp.concatenate(split_low(grad_block[:, : 3 * own_cols]), axis=1)
    cols_send = cols_send.reshape(n_ctx, attn_rows, 6 * own_cols)
    out_part = jnp.stack(split_low(grad_block[:, 3 * own_cols :]), axis=1)
    out_part = out_part.reshape(-1, 2, 2, n_ctx, attn_rows).transpose(3, 4, 2, 1, 0)
    out_part = out_part.reshape(n_ctx, attn_rows, 2 * own_cols)
    grad_send = jnp.concatenate([cols_send, out_part], axis=2).reshape(n_ctx, -1, own_cols)
    small_send = jnp.concatenate([vec_part, grad_send], axis=1)
    out_pack = grad_normed.reshape(n_ctx, own_len, width)
    out_pack, small_send, shard = lax.optimization_barrier((out_pack, small_send, shard))
    shard = jnp.broadcast_to(shard, (n_ctx,) + shard.shape)
    shard = trade(jnp.concatenate([shard, small_send], axis=1), ctx_axes)
    out_pack, shard = lax.optimization_barrier((out_pack, shard))
    other = swap(shard)
    out_pack = trade(out_pack, ctx_axes)

    (current,) = call(
        newton_schulz_kernel,
        [low(*own.shape)],
        [shard, other, own],
        20 * width * width * width,
        scratch=[
            pltpu.VMEM((width, width), wide_type),
            pltpu.VMEM((width, width), low_type),
            pltpu.VMEM((width, width), low_type),
            pltpu.VMEM((width, width), low_type),
            pltpu.VMEM(own.shape, wide_type),
        ],
        flags=[owns_ffn, core, ctx, chip == attn_owners[3]],
        name="newton_schulz",
    )
    small_sent, current = lax.optimization_barrier((shard[:, width // 2 :], current))
    out_sum = small_sent[:, :vec_lines].astype(wide_type).sum(axis=0)
    vec_sum = out_sum.reshape(-1)[:n_sent].reshape(n_chip, 2, 2, n_vec).sum(axis=2)
    vec_kept = lax.dynamic_index_in_dim(vec_sum, core, axis=1, keepdims=False)
    vec_given = lax.dynamic_index_in_dim(vec_sum, 1 - core, axis=1, keepdims=False)
    attn_grad = small_sent[:, vec_lines:].reshape(n_ctx, attn_rows, width).astype(wide_type)
    cols_grad = attn_grad[:, :, : 3 * own_cols] + attn_grad[:, :, 3 * own_cols : 6 * own_cols]
    cols_grad = cols_grad.reshape(n_ctx, attn_rows, 3, own_cols).transpose(2, 1, 0, 3)
    out_part = attn_grad[:, :, 6 * own_cols :].reshape(n_chip, attn_rows, 2, 2, -1).sum(axis=3)
    out_part = out_part.transpose(2, 0, 1, 3)
    out_kept = lax.dynamic_index_in_dim(out_part, core, axis=0, keepdims=False)
    out_given = lax.dynamic_index_in_dim(out_part, 1 - core, axis=0, keepdims=False)
    both = jnp.concatenate([vec_given, out_given.reshape(n_chip, -1)], axis=1)
    both = swap(both)
    vec_sum = vec_kept + both[:, :n_vec]
    out_part = pair(out_kept, both[:, n_vec:].reshape(out_given.shape)).transpose(1, 2, 0, 3)
    out_part = out_part.reshape(n_chip, attn_rows, own_cols)
    vec_row = jnp.concatenate(split_low(vec_sum), axis=1)
    vec_row = jnp.pad(vec_row[:, None], ((0, 0), (0, attn_rows - 1), (0, width - 2 * own_cols - 2 * n_vec)))
    last_rows = jnp.concatenate([*split_low(out_part), vec_row], axis=2)
    back = jnp.concatenate([current.reshape(n_chip, ffn_rows, width), last_rows], axis=1)
    back, out_pack = lax.optimization_barrier((back, out_pack))
    back = trade(back, chip_axes)
    grad_normed = jnp.sum(out_pack.astype(wide_type), axis=0)
    own_mean = jnp.mean(own_x, axis=-1, keepdims=True)
    own_centered = own_x - own_mean
    own_var = jnp.mean(own_centered * own_centered, axis=-1, keepdims=True)
    own_std = lax.rsqrt(own_var + norm_epsilon)
    own_normed = own_centered * own_std
    grad_center = (
        grad_normed
        - jnp.mean(grad_normed, axis=-1, keepdims=True)
        - own_normed * jnp.mean(grad_normed * own_normed, axis=-1, keepdims=True)
    )
    input_grad = (own_dy + own_std * grad_center)[None]
    outputs = (own_x + branch + bias_o + bias_down).astype(low_type)[None]
    back, input_grad, outputs = lax.optimization_barrier((back, input_grad, outputs))
    back = back.astype(wide_type)
    ortho_ffn = jnp.stack([back[owner, :ffn_rows] for owner in ffn_owners])
    ortho_attn = jnp.stack([back[owner, :attn_rows] for owner in attn_owners])
    last_rows = back[:, ffn_rows:]
    vec_grad = last_rows[:, 0, 2 * own_cols : 2 * own_cols + 2 * n_vec].reshape(n_chip, 2, n_vec)
    vec_grad = vec_grad.sum(axis=(0, 1))
    out_part = last_rows[:, :, :own_cols] + last_rows[:, :, own_cols : 2 * own_cols]
    out_part = out_part.transpose(1, 0, 2).reshape(1, attn_rows, width)
    attn_grad = jnp.concatenate([cols_grad.reshape(3, attn_rows, width), out_part], axis=0)
    attn_moment_new = momentum_decay * attn_moment + attn_grad
    attn_steps = jnp.array([1.0, 1.0, 1.0, 2.0], wide_type)
    ffn_steps = jnp.array([math.sqrt(FF / D), 2.0], wide_type)
    attn_new = (
        attn_weights * (1.0 - learn_rate * weight_decay)
        - learn_rate * attn_steps[:, None, None] * ortho_attn
    )
    ffn_new = (
        ffn_weights * (1.0 - learn_rate * weight_decay)
        - learn_rate * ffn_steps[:, None, None] * ortho_ffn
    )
    vec_first_new = beta_first * vec_first + (1.0 - beta_first) * vec_grad
    vec_second_new = beta_second * vec_second + (1.0 - beta_second) * vec_grad * vec_grad
    first_hat = vec_first_new / (1.0 - beta_first**STEP)
    second_hat = vec_second_new / (1.0 - beta_second**STEP)
    vec_new = vectors - vector_rate * first_hat / (jnp.sqrt(second_hat) + adam_epsilon)
    return (
        outputs,
        input_grad,
        attn_grad,
        ffn_grad,
        vec_grad,
        attn_moment_new,
        ffn_moment_new,
        attn_new,
        ffn_new,
        vec_first_new,
        vec_second_new,
        vec_new,
    )


def solution(mesh):
    names = dp_axes + ctx_axes
    fine = Mesh(mesh.devices.reshape(2, 4, 2, 2, 4), names)
    in_specs = (
        P(dp_axes, ctx_axes, None),
        P(dp_axes, ctx_axes, None),
        P(None, dp_axes + ctx_axes, None),
        P(None, dp_axes + ctx_axes, None),
        P(dp_axes + ctx_axes),
        P(None, dp_axes + ctx_axes, None),
        P(None, dp_axes + ctx_axes, None),
        P(dp_axes + ctx_axes),
        P(dp_axes + ctx_axes),
    )
    out_specs = (
        P(dp_axes, ctx_axes, None),
        P(dp_axes, ctx_axes, None),
        P(None, dp_axes + ctx_axes, None),
        P(None, dp_axes + ctx_axes, None),
        P(dp_axes + ctx_axes),
        P(None, dp_axes + ctx_axes, None),
        P(None, dp_axes + ctx_axes, None),
        P(None, dp_axes + ctx_axes, None),
        P(None, dp_axes + ctx_axes, None),
        P(dp_axes + ctx_axes),
        P(dp_axes + ctx_axes),
        P(dp_axes + ctx_axes),
    )
    return jax.shard_map(local, mesh=fine, in_specs=in_specs, out_specs=out_specs, check_vma=False)
```

```python
import math

import jax
import jax.numpy as jnp
from jax import lax
from jax.experimental import pallas as pl
from jax.experimental.pallas import tpu as pltpu
from jax.sharding import Mesh
from jax.sharding import PartitionSpec as P

D = 1024
FF = 4096
HEADS = 16
HD = 64
ROT = 16
ITERS = 3
STEP = 10


norm_epsilon = 1e-05
quintic_one = 3.4445
quintic_two = -4.775
quintic_three = 2.0315
momentum_decay = 0.95
learn_rate = 0.4
weight_decay = 0.01
beta_first = 0.9
beta_second = 0.95
vector_rate = 0.05
adam_epsilon = 1e-08

low_type = jnp.bfloat16
wide_type = jnp.float32
dp_axes = ("z_lo", "x", "core")
ctx_axes = ("z_hi", "y")
chip_axes = ("z_lo", "x")
ffn_owners = (0, 6)
attn_owners = (1, 3, 5, 7)


def trade(blocks, axes):
    return lax.all_to_all(blocks, axes, split_axis=0, concat_axis=0, tiled=True)


def spread(block, axes):
    return trade(jnp.broadcast_to(block, (lax.axis_size(axes),) + block.shape), axes)


def collect(partials, axes):
    return jnp.sum(trade(partials.astype(low_type), axes).astype(wide_type), axis=0)


def swap(block):
    return lax.ppermute(block, "core", [(0, 1), (1, 0)])


def halve(pairs):
    core = lax.axis_index("core")
    kept = lax.dynamic_index_in_dim(pairs, core, axis=0, keepdims=False)
    given = lax.dynamic_index_in_dim(pairs, 1 - core, axis=0, keepdims=False)
    return kept.astype(wide_type) + swap(given).astype(wide_type)


def pair(mine, other):
    first = lax.axis_index("core") == 0
    return jnp.stack([jnp.where(first, mine, other), jnp.where(first, other, mine)])


def split_low(wide):
    high = lax.reduce_precision(wide, 8, 7)
    return high.astype(low_type), (wide - high).astype(low_type)


def dot(left, right):
    return jnp.dot(left, right, preferred_element_type=wide_type)


def dot_nt(left, right):
    return lax.dot_general(
        left, right, (((1,), (1,)), ((), ())), preferred_element_type=wide_type
    )


def dot_tn(left, right):
    return lax.dot_general(
        left, right, (((0,), (0,)), ((), ())), preferred_element_type=wide_type
    )


def rope_tables(length, heads):
    lane = lax.rem(jnp.arange(heads * HD, dtype=jnp.int32), HD)
    half_rot = ROT // 2
    inv_freq = 10000.0 ** (-(lax.rem(lane, half_rot).astype(wide_type) * 2.0) / ROT)
    angles = jnp.arange(length, dtype=jnp.int32).astype(wide_type)[:, None] * inv_freq[None, :]
    keep = jnp.where(lane < ROT, jnp.cos(angles), 1.0)
    sines = jnp.sin(angles)
    ahead = jnp.where(lane < half_rot, -sines, 0.0)
    behind = jnp.where((lane >= half_rot) & (lane < ROT), sines, 0.0)
    return keep, ahead, behind


def turned(rows, tables):
    half_rot = ROT // 2
    cols = rows.shape[1]
    ahead = pltpu.roll(rows, cols - half_rot, 1)
    behind = pltpu.roll(rows, half_rot, 1)
    return ahead * tables[1] + behind * tables[2]


def attention_kernel(
    flags_ref, qkv_ref, mixed_grad_ref, keep_ref, ahead_ref, behind_ref, first_far, dy_far, mixed_ref, grad_ref, g_kept_ref,
    g_given_ref, k_sum, v_sum, g_all, first_ref, dy_ref, sems
):
    length, cols = keep_ref.shape
    heads = cols // HD
    scale = HD ** (-0.5)
    tables = (keep_ref[...], ahead_ref[...], behind_ref[...])
    first_copy = pltpu.make_async_copy(first_far, first_ref, sems.at[0])
    dy_copy = pltpu.make_async_copy(dy_far, dy_ref, sems.at[1])
    first_copy.start()
    dy_copy.start()
    q_rot = qkv_ref[:, :cols]
    k_rot = qkv_ref[:, cols : 2 * cols]
    v_low = qkv_ref[:, 2 * cols :]
    k_sum[...] = jnp.zeros_like(k_sum)
    v_sum[...] = jnp.zeros_like(v_sum)
    block = 256
    for start in range(0, length, block):
        stop = start + block
        q_grads = []
        for head in range(heads):
            lanes = slice(head*HD, (head+1)*HD)
            q_now, k_now, v_now = q_rot[start:stop, lanes], k_rot[:stop, lanes], v_low[:stop, lanes]
            grad_t = mixed_grad_ref[lanes, start:stop]
            raw = dot_nt(k_now, q_now) * scale
            key_pos = lax.broadcasted_iota(jnp.int32, (stop, block), 0)
            query_pos = lax.broadcasted_iota(jnp.int32, (stop, block), 1) + start
            scores = jnp.where(key_pos <= query_pos, raw, -1e30)
            expo = jnp.exp(scores - jnp.max(scores, axis=0, keepdims=True))
            probs = expo * (1.0 / jnp.sum(expo, axis=0, keepdims=True))
            probs_low = probs.astype(low_type)
            mixed_ref[lanes, start:stop] = dot_tn(v_now, probs_low).astype(low_type)
            grad_probs = dot(v_now, grad_t)
            inner = jnp.sum(probs * grad_probs, axis=0, keepdims=True)
            grad_raw = (probs * (grad_probs - inner) * scale).astype(low_type)
            q_grads.append(dot_tn(k_now, grad_raw))
            k_sum[head, :stop, :] += dot(grad_raw, q_now)
            v_sum[head, :stop, :] += dot_nt(probs_low, grad_t)
        grad_q = jnp.concatenate(q_grads, axis=0).T
        part = tuple(table[start:stop] for table in tables)
        grad_ref[start:stop, :cols] = (grad_q * part[0] - turned(grad_q, part)).astype(low_type)
    grad_k = jnp.concatenate([k_sum[head] for head in range(heads)], axis=1)
    grad_v = jnp.concatenate([v_sum[head] for head in range(heads)], axis=1)
    grad_ref[:, cols:2*cols] = (grad_k * tables[0] - turned(grad_k, tables)).astype(low_type)
    grad_ref[:, 2*cols:] = grad_v.astype(low_type)
    first_copy.wait()
    dy_copy.wait()
    for start in range(0, first_ref.shape[0], block):
        g_all[start : start + block, : 3 * cols] = dot(
            first_ref[start : start + block], grad_ref[...]
        ).astype(low_type)
        g_all[start : start + block, 3 * cols :] = dot(
            mixed_ref[...], dy_ref[:, start : start + block]
        ).T.astype(low_type)
    chips, part = g_kept_ref.shape[:2]
    core = flags_ref[0]
    for chip in range(chips):
        for place, out_ref in ((core, g_kept_ref), (1 - core, g_given_ref)):
            out_ref[chip] = g_all[pl.ds(pl.multiple_of((2 * chip + place) * part, part), part)]


def vmem_specs(count):
    return [pl.BlockSpec(memory_space=pltpu.VMEM)] * count


def call(kernel, outs, args, flops, scratch=(), flags=None, name=None, views={}, far=(), far_out=()):
    specs, size = [], 0
    for index, each in enumerate(args):
        block, place = views.get(index, (each.shape, (0,) * each.ndim))
        if index in far:
            specs.append(pl.BlockSpec(memory_space=pl.ANY))
        else:
            specs.append(pl.BlockSpec(block, lambda step, place=place: place))
        size += math.prod(block) * each.dtype.itemsize
    size += sum(math.prod(each.shape) * each.dtype.itemsize for each in outs)
    args = list(args)
    if flags is not None:
        specs = [pl.BlockSpec(memory_space=pltpu.SMEM)] + specs
        args = [jnp.stack([jnp.asarray(flag, jnp.int32) for flag in flags])] + args
    return pl.pallas_call(
        kernel,
        grid=(1,),
        out_shape=tuple(outs),
        in_specs=specs,
        out_specs=tuple(
            pl.BlockSpec(memory_space=pl.ANY)
            if index in far_out
            else pl.BlockSpec(each.shape, lambda step, rank=len(each.shape): (0,) * rank)
            for index, each in enumerate(outs)
        ),
        scratch_shapes=list(scratch),
        compiler_params=pltpu.CompilerParams(vmem_limit_bytes=60 * 1024 * 1024),
        cost_estimate=pl.CostEstimate(flops=flops, bytes_accessed=size, transcendentals=0),
        name=name,
    )(*args)


def wide(*shape):
    return jax.ShapeDtypeStruct(shape, wide_type)


def low(*shape):
    return jax.ShapeDtypeStruct(shape, low_type)


def normalized(rows):
    rows = rows.astype(wide_type)
    centered = rows - jnp.mean(rows, axis=-1, keepdims=True)
    variance = jnp.mean(centered * centered, axis=-1, keepdims=True)
    return centered * lax.rsqrt(variance + norm_epsilon)


def pack_kernel(x_ref, weights_ref, moment_ref, vec_ref, out_ref):
    tokens = x_ref.shape[0]
    cols = weights_ref.shape[2] // out_ref.shape[0]
    for target in range(out_ref.shape[0]):
        lanes = slice(target * cols, (target + 1) * cols)
        out_ref[target, :tokens] = x_ref[...]
        vec = jnp.broadcast_to(vec_ref[...], (weights_ref.shape[1], vec_ref.shape[1]))
        weights = [weights_ref[index, :, lanes] for index in range(4)]
        blank = jnp.zeros((weights_ref.shape[1], 4 * cols - vec_ref.shape[1]), wide_type)
        moments = [moment_ref[index, :, lanes] for index in range(3)]
        highs = [moment.astype(low_type).astype(wide_type) for moment in moments]
        lows = [moment - high for moment, high in zip(moments, highs)]
        rest = jnp.zeros((weights_ref.shape[1], 2 * cols), wide_type)
        upper = jnp.concatenate([*weights, vec, blank], axis=1)
        lower = jnp.concatenate([*highs, *lows, rest], axis=1)
        out_ref[target, tokens:] = jnp.concatenate([upper, lower], axis=0).astype(low_type)


def owners_kernel(ffn_moment_ref, ffn_grad_ref, moment_ref, grad_ref, out_ref, ffn_new_ref):
    for index, owner in enumerate(ffn_owners):
        rows = momentum_decay * ffn_moment_ref[index] + ffn_grad_ref[index]
        ffn_new_ref[index] = rows
        out_ref[owner] = rows.astype(low_type)
    block = momentum_decay * moment_ref[...] + grad_ref[...]
    cols, rows = block.shape[1] // 4, 8
    groups = block.shape[0] // rows
    blank = jnp.zeros((out_ref.shape[1] - rows, out_ref.shape[2]), wide_type)
    for index, owner in enumerate(attn_owners):
        lanes = slice(index * cols, (index + 1) * cols)
        parts = [block[rows * group : rows * (group + 1), lanes] for group in range(groups)]
        filled = jnp.concatenate([jnp.concatenate(parts, axis=1), blank], axis=0)
        out_ref[owner] = filled.astype(low_type)
    for owner in range(out_ref.shape[0]):
        if owner not in ffn_owners + attn_owners:
            out_ref[owner] = jnp.zeros(out_ref.shape[1:], low_type)


def unpack_kernel(flags_ref, mine_ref, other_ref, dy_ref, qkv_ref, out_ref):
    half, tokens, cols = 32, dy_ref.shape[0], out_ref.shape[2] // 8
    first = flags_ref[0] == 0
    mine, other = mine_ref[:, :half], other_ref[:, :half]
    for core, part in enumerate((jnp.where(first, mine, other), jnp.where(first, other, mine))):
        for upper in range(2):
            lanes = part[:, :, upper * 4 * cols : (upper + 1) * 4 * cols]
            qkv_ref[:, core, upper * half : (upper + 1) * half] = lanes[:, :, : 3 * cols]
            for group in range(2):
                place = (4 * core + 2 * upper + group) * cols
                out_ref[:, tokens : tokens + 16, place : place + cols] = lanes[
                    :, 16 * group : 16 * (group + 1), 3 * cols :
                ]
    rows = []
    for ref in (mine_ref, other_ref):
        last = ref[:, half:].astype(wide_type)
        rows.append(jnp.where(first, last[:, 1:2], last[:, 2:3]))
    blank = jnp.zeros((out_ref.shape[0], 14, out_ref.shape[2]), wide_type)
    pair_rows = [jnp.where(first, rows[0], rows[1]), jnp.where(first, rows[1], rows[0])]
    out_ref[:, tokens + 16 :] = jnp.concatenate([*pair_rows, blank], axis=1).astype(low_type)
    for target in range(out_ref.shape[0]):
        out_ref[target, :tokens] = dy_ref[...]


def qkv_kernel(
    x_ref, keep_ref, ahead_ref, behind_ref, gain_ref, shift_ref, w_ref, bias_ref, first_ref, out_ref
):
    cols = keep_ref.shape[1]
    tables = (keep_ref[...], ahead_ref[...], behind_ref[...])
    normed = normalized(x_ref[...].reshape(-1, x_ref.shape[2]))
    wide_first = normed * gain_ref[...] + shift_ref[...]
    first = wide_first.astype(low_type)
    first_ref[...] = wide_first.T.astype(low_type)
    rows = dot(first, w_ref[...]) + bias_ref[...]
    for index in range(2):
        part = rows[:, index * cols : (index + 1) * cols]
        out_ref[:, index * cols : (index + 1) * cols] = (
            part * tables[0] + turned(part, tables)
        ).astype(low_type)
    out_ref[:, 2 * cols :] = rows[:, 2 * cols :].astype(low_type)


def ffn_forward_kernel(x_ref, gain_ref, shift_ref, up_ref, bias_ref, second_ref, hidden_ref, slope_ref):
    sources, tokens, width = x_ref.shape
    for source in range(sources):
        second_ref[source * tokens : (source + 1) * tokens] = (
            normalized(x_ref[source]) * gain_ref[...] + shift_ref[...]
        ).astype(low_type)
    for index in range(2):
        pre = dot_nt(up_ref[:, index].reshape(-1, width), second_ref[...]) + bias_ref[index]
        chance = 0.5 * (1.0 + lax.erf(pre * math.sqrt(0.5)))
        density = jnp.exp(-0.5 * pre * pre) * (1.0 / math.sqrt(2.0 * math.pi))
        hidden_ref[index] = (pre * chance).astype(low_type)
        slope_ref[index] = chance + pre * density


def ffn_backward_kernel(
    flags_ref, pack_ref, rows_ref, slope_ref, second_ref, hidden_ref, dy_ref, grad_up_ref, kept_ref,
    given_ref, g_bias_ref, w_out_ref, mixed_grad_ref, dy, down, slope, second, hidden, out_rows, sems
):
    chips, units, width = kept_ref.shape
    units = units // 2
    sources, tokens = pack_ref.shape[0], pack_ref.shape[1] - 32
    copies = []

    def fetch(source, target):
        copy = pltpu.make_async_copy(source, target, sems.at[len(copies)])
        copy.start()
        copies.append(copy)
        return copy

    parts = []
    for source in range(sources):
        parts.append(
            fetch(pack_ref.at[source, pl.ds(0, tokens)], dy.at[pl.ds(source * tokens, tokens)])
        )
    parts.append(fetch(rows_ref.at[:, :, pl.ds(units, units)], down))
    slope_copy = fetch(slope_ref, slope)
    second_copy = fetch(second_ref, second)
    hidden_copy = fetch(hidden_ref, hidden)
    out_copy = fetch(pack_ref.at[:, pl.ds(tokens, 16)], out_rows)
    for part in parts:
        part.wait()
    back_copy = fetch(dy, dy_ref)
    ones = jnp.ones((8, dy.shape[0]), low_type)
    for index in range(2):
        grad_hidden = dot_nt(down[:, index].reshape(-1, width), dy[...])
        if index == 0:
            slope_copy.wait()
        grad_up = (grad_hidden * slope[index]).astype(low_type)
        grad_up_ref[index] = grad_up
        g_bias_ref[index] = dot_nt(ones, grad_up)
        if index == 0:
            second_copy.wait()
        g_up = dot(grad_up, second[...]).astype(low_type).reshape(chips, units, width)
        if index == 0:
            hidden_copy.wait()
        g_down = dot(hidden[index], dy[...]).astype(low_type).reshape(chips, units, width)

        @pl.when(flags_ref[0] == index)
        def _():
            kept_ref[:, :units] = g_up
            kept_ref[:, units:] = g_down

        @pl.when(flags_ref[0] != index)
        def _():
            given_ref[:, :units] = g_up
            given_ref[:, units:] = g_down

    out_copy.wait()
    cols = width // sources
    for source in range(sources):
        for group in range(8):
            w_out_ref[16 * group : 16 * (group + 1), source * cols : (source + 1) * cols] = out_rows[
                source, :, group * cols : (group + 1) * cols
            ]
    mixed_grad_ref[...] = dot_nt(w_out_ref[...], dy[...]).astype(low_type)
    back_copy.wait()


def normal_kernel(
    grad_ref, grad_up_ref, x_ref, w_ref, rows_ref, gain_one_ref, gain_two_ref, out_ref, sums_ref
):
    first = dot_nt(grad_ref[...], w_ref[...])
    second = 0.0
    for index in range(2):
        up = rows_ref[:, index].reshape(-1, first.shape[1])
        second = second + dot_tn(grad_up_ref[index], up)
    normed = normalized(x_ref[...].reshape(first.shape))
    out_ref[...] = (first * gain_one_ref[...] + second * gain_two_ref[...]).astype(low_type)
    terms = (first * normed, first, second * normed, second)
    sums = jnp.concatenate([jnp.sum(term, axis=0, keepdims=True) for term in terms], axis=0)

    @pl.when(pl.program_id(0) == 0)
    def _():
        sums_ref[...] = jnp.zeros_like(sums_ref)

    sums_ref[...] += sums


def branch_kernel(hidden_ref, mixed_ref, rows_ref, w_out_ref, out_ref, mark_ref):
    total = dot_tn(mixed_ref[...], w_out_ref[...])
    for index in range(2):
        down = rows_ref[:, index].reshape(-1, total.shape[1])
        total = total + dot_tn(hidden_ref[index], down)
    out_ref[...] = total
    mark_ref[...] = total[:8, :128]


def gram_kernel(flags_ref, own_ref, other_ref, out_ref):
    half, cols = out_ref.shape[1:]
    lanes = pl.ds(pl.multiple_of(flags_ref[0] * half, half), half)
    rows = dot_tn(own_ref[:, lanes], own_ref[...]) + dot_tn(other_ref[:, lanes], other_ref[...])
    for index in range(out_ref.shape[0]):
        out_ref[index] = rows[:, index * cols : (index + 1) * cols].astype(low_type)


def call_rows(kernel, outs, args, blocks, flops, steps, name):
    arrays = list(args) + list(outs)
    specs, size = [], 0
    for each, given in zip(arrays, blocks):
        shape, place = given or (each.shape, lambda step, rank=len(each.shape): (0,) * rank)
        specs.append(pl.BlockSpec(shape, place))
        size += math.prod(shape) * each.dtype.itemsize * (steps if given else 1)
    return pl.pallas_call(
        kernel,
        grid=(steps,),
        out_shape=tuple(outs),
        in_specs=specs[: len(args)],
        out_specs=tuple(specs[len(args) :]),
        compiler_params=pltpu.CompilerParams(vmem_limit_bytes=60 * 1024 * 1024),
        cost_estimate=pl.CostEstimate(flops=flops, bytes_accessed=size, transcendentals=0),
        name=name,
    )(*args)


def newton_schulz_kernel(
    flags_ref, mine_ref, other_ref, rows_ref, out_ref, gram_ref, low_ref, mixer_ref, start_ref, current_ref
):
    width = rows_ref.shape[1]
    half = width // 2
    block = 512
    chips = 8
    attn_rows, units = 8, rows_ref.shape[0] // chips
    core, ctx = flags_ref[1], flags_ref[2]
    cols = mine_ref.shape[2]
    part = half // chips

    @pl.when(flags_ref[0] == 1)
    def _():
        for source in range(mine_ref.shape[0]):
            lanes = slice(source * cols, (source + 1) * cols)
            for place, ref in ((core, mine_ref), (1 - core, other_ref)):
                rows = pl.ds(pl.multiple_of(place * half, half), half)
                gram_ref[rows, lanes] = ref[source, :half].astype(wide_type)
        total = jnp.zeros((1, 1), wide_type)
        for start in range(0, width, 256):
            square = gram_ref[start : start + 256, start : start + 256]
            diagonal = lax.broadcasted_iota(jnp.int32, square.shape, 0) == lax.broadcasted_iota(
                jnp.int32, square.shape, 1
            )
            total = total + jnp.sum(jnp.where(diagonal, square, 0.0), keepdims=True)
        factor = 1.0 / (jnp.sqrt(total) + 1e-07)
        gram_ref[...] = gram_ref[...] * (factor * factor)
        current_ref[...] = rows_ref[...].astype(wide_type) * factor

    @pl.when(flags_ref[0] == 0)
    def _():
        for source in range(mine_ref.shape[0]):
            lanes = slice(source * cols, (source + 1) * cols)
            for chip in range(chips):
                for place, ref in ((core, mine_ref), (1 - core, other_ref)):
                    rows = pl.ds(pl.multiple_of((2 * chip + place) * part, part), part)
                    gram_ref[rows, lanes] = ref[source, chip * part : (chip + 1) * part].astype(wide_type)
        raw = gram_ref[...]
        factor = 1.0 / (jnp.sqrt(jnp.sum(raw * raw, keepdims=True)) + 1e-07)
        start_ref[...] = (raw * factor).astype(low_type)
        blank = jnp.zeros((units - attn_rows, width), wide_type)
        for chip in range(chips):
            place = pl.multiple_of((2 * chip + core) * part + attn_rows * ctx, attn_rows)
            rows = gram_ref[pl.ds(place, attn_rows)] * factor
            current_ref[units * chip : units * (chip + 1)] = jnp.concatenate([rows, blank])

        @pl.when(flags_ref[3] == 1)
        def _():
            row = lax.broadcasted_iota(jnp.int32, current_ref.shape, 0)
            inner = lax.rem(row, units)
            place = (lax.div(row, units) * 2 + core) * part + attn_rows * ctx + inner
            lane = lax.broadcasted_iota(jnp.int32, current_ref.shape, 1)
            current_ref[...] = jnp.where((lane == place) & (inner < attn_rows), 1.0, 0.0)

        for start in range(0, width, 256):
            lanes = slice(start, start + 256)
            gram_ref[lanes] = dot_tn(start_ref[:, lanes], start_ref[...])

    def mix(index, carry):
        rows = pl.ds(pl.multiple_of(index * block, block), block)
        square = dot(low_ref[rows], low_ref[...])
        mixer_ref[rows] = (quintic_two * gram_ref[rows] + quintic_three * square).astype(low_type)
        return carry

    def advance(index, carry):
        rows = pl.ds(pl.multiple_of(index * block, block), block)
        turn = quintic_one * gram_ref[rows] + dot(low_ref[rows], mixer_ref[...])
        gram_ref[rows] = quintic_one * turn + dot(turn.astype(low_type), mixer_ref[...])
        return carry

    def times(rows, matrix_ref):
        return dot(rows.astype(low_type), matrix_ref[...])

    def factor_times(rows):
        return quintic_one * rows + times(rows, mixer_ref)

    for repeat in range(2):
        low_ref[...] = gram_ref[...].astype(low_type)
        lax.fori_loop(0, width // block, mix, 0)
        current_ref[...] = factor_times(current_ref[...])
        if repeat == 0:
            lax.fori_loop(0, width // block, advance, 0)

    def third_gram_times(rows):
        return factor_times(times(factor_times(rows), low_ref))

    current = current_ref[...]
    once = third_gram_times(current)
    twice = third_gram_times(once)
    current_ref[...] = quintic_one * current + quintic_two * once + quintic_three * twice
    out_ref[...] = current_ref[...].astype(low_type)

    @pl.when(flags_ref[3] == 1)
    def _():
        out_ref[...] = dot_nt(out_ref[...], start_ref[...]).astype(low_type)


def local(
    inputs,
    out_grad,
    attn_weights,
    ffn_weights,
    vectors,
    attn_moment,
    ffn_moment,
    vec_first,
    vec_second,
):
    seq_dev, own_len, width = inputs.shape
    n_ctx = lax.axis_size(ctx_axes)
    n_dp = lax.axis_size(dp_axes)
    n_chip = lax.axis_size(chip_axes)
    ctx = lax.axis_index(ctx_axes)
    core = lax.axis_index("core")
    chip = lax.axis_index(chip_axes)
    length = own_len * n_ctx
    mats, attn_rows = attn_weights.shape[:2]
    ffn_rows = ffn_weights.shape[1]
    hidden_units = n_dp * ffn_rows
    n_vec = vectors.shape[0]
    own_heads = HEADS // n_ctx
    own_cols = own_heads * HD
    block_cols = mats * own_cols
    block_rows = n_ctx * attn_rows
    half = block_rows // 2

    (first_pack,) = call(
        pack_kernel,
        [low(n_ctx, own_len + 2 * attn_rows, width)],
        [
            inputs[0],
            attn_weights,
            attn_moment,
            jnp.pad(vectors[None], ((0, 0), (0, 128 - n_vec))),
        ],
        0,
        name="pack",
    )
    first_pack = trade(first_pack, ctx_axes)
    ffn_all = lax.all_gather(ffn_weights.astype(low_type).reshape(2 * ffn_rows, width), dp_axes)
    ffn_all = ffn_all.reshape(n_chip, 2, 2 * ffn_rows, width)
    x_view = ((n_ctx, own_len, width), (0, 0, 0))
    up_view = ((n_chip, 2, ffn_rows, width), (0, 0, 0, 0))
    down_view = ((n_chip, 2, ffn_rows, width), (0, 0, 1, 0))
    tables = rope_tables(length, own_heads)
    first_pack, tables = lax.optimization_barrier((first_pack, tables))
    small = first_pack[:, own_len : own_len + attn_rows]
    moment_cols = first_pack[:, own_len + attn_rows :].astype(wide_type)
    moment_cols = moment_cols[:, :, : 3 * own_cols] + moment_cols[:, :, 3 * own_cols : 6 * own_cols]
    moment_cols = moment_cols.reshape(block_rows, 3 * own_cols)

    attn_block = small[:, :, :block_cols].reshape(block_rows, block_cols)
    vec_block = small[:, 0, block_cols : block_cols + n_vec].reshape(1, n_ctx * n_vec)
    vec_block = jnp.pad(vec_block, ((0, 0), (0, width - n_ctx * n_vec)))
    pack = jnp.concatenate(
        [
            jnp.concatenate([attn_block[:half], attn_block[half:]], axis=1),
            vec_block,
        ],
        axis=0,
    )
    out_moment = jnp.stack(split_low(attn_moment[3])).reshape(2, attn_rows, n_chip, 2, -1)
    out_moment = out_moment.transpose(2, 3, 0, 1, 4).reshape(n_chip, 2, width)
    out_moment = jnp.pad(out_moment, ((0, 0), (0, 5), (0, 0)))
    pack = jnp.broadcast_to(pack, (n_chip,) + pack.shape)
    pack = trade(jnp.concatenate([pack, out_moment], axis=1), chip_axes)
    pack, moment_cols = lax.optimization_barrier((pack, moment_cols))
    other_pack = swap(pack)
    w_qkv, dy_pack = call(
        unpack_kernel,
        [low(n_chip, 2, block_rows, 3 * own_cols), low(n_ctx, own_len + 32, width)],
        [pack, other_pack, out_grad[0]],
        0,
        flags=[core],
        name="unpack",
    )
    w_qkv = w_qkv.reshape(width, 3 * own_cols)
    dy_pack = trade(dy_pack, ctx_axes)

    vec_rows = [part[:, half, : n_ctx * n_vec] for part in (pack, other_pack)]
    vec_wide = pair(*vec_rows).transpose(1, 0, 2).reshape(-1).astype(wide_type)
    pieces = [vec_wide[index * width : (index + 1) * width] for index in range(9)]
    gain_one, bias_one, gain_two, bias_two, bias_q, bias_k, bias_v, bias_o, bias_down = pieces
    bias_qkv = jnp.concatenate(
        [
            lax.dynamic_slice(piece, (ctx * own_cols,), (own_cols,))
            for piece in (bias_q, bias_k, bias_v)
        ]
    )
    bias_up = lax.dynamic_index_in_dim(
        vec_wide[9 * width :].reshape(n_chip, 2, n_ctx, ffn_rows), ctx, axis=2, keepdims=False
    )
    bias_up = bias_up.transpose(1, 0, 2).reshape(2, n_chip * ffn_rows, 1)
    steps = n_ctx // 2

    def row_block(cols):
        return (length // steps, cols), lambda step: (step, 0)

    x_rows = (n_ctx // steps, own_len, width), lambda step: (step, 0, 0)
    turned_block = (width, length // steps), lambda step: (0, step)
    first_turned, qkv = call_rows(
        qkv_kernel,
        [low(width, length), low(length, 3 * own_cols)],
        [first_pack, *tables, gain_one[None], bias_one[None], w_qkv, bias_qkv[None]],
        [x_rows, *[row_block(own_cols)] * 3, *[None] * 4, turned_block, row_block(3 * own_cols)],
        6 * own_cols * length * width,
        steps,
        "qkv",
    )

    second_in, hidden, slope = call(
        ffn_forward_kernel,
        [low(length, width), low(2, hidden_units // 2, length), wide(2, hidden_units // 2, length)],
        [first_pack, gain_two[None], bias_two[None], ffn_all, bias_up],
        2 * hidden_units * length * width,
        views={0: x_view, 3: up_view},
        name="forward",
    )
    dy_pack, qkv, hidden = lax.optimization_barrier((dy_pack, qkv, hidden))
    dy_low, grad_up, kept, given, grad_b_up, w_out, mixed_grad = call(
        ffn_backward_kernel,
        [
            low(length, width),
            low(2, hidden_units // 2, length),
            low(n_chip, 2 * ffn_rows, width),
            low(n_chip, 2 * ffn_rows, width),
            wide(2, 8, n_chip * ffn_rows),
            low(own_cols, width),
            low(own_cols, length),
        ],
        [dy_pack, ffn_all, slope, second_in, hidden],
        (6 * hidden_units + 2 * own_cols) * length * width,
        scratch=[
            pltpu.VMEM((length, width), low_type),
            pltpu.VMEM((n_chip, 2, ffn_rows, width), low_type),
            pltpu.VMEM((2, hidden_units // 2, length), wide_type),
            pltpu.VMEM((length, width), low_type),
            pltpu.VMEM((2, hidden_units // 2, length), low_type),
            pltpu.VMEM((n_ctx, 16, width), low_type),
            pltpu.SemaphoreType.DMA((14,)),
        ],
        flags=[core],
        far=range(5),
        far_out=(0,),
        name="backward",
    )
    ffn_part = (kept.astype(wide_type) + swap(given).astype(wide_type)).astype(low_type)
    ffn_part, mixed_grad = lax.optimization_barrier((ffn_part, mixed_grad))
    out_moment = dy_pack[:, own_len + 16 : own_len + 18].reshape(n_ctx, 2, 2, attn_rows, -1).astype(wide_type).sum(axis=2)
    out_moment = out_moment.transpose(3, 1, 0, 2).reshape(block_rows, own_cols)
    moment_block = jnp.concatenate([moment_cols, out_moment], axis=1)
    ffn_parts = trade(ffn_part, chip_axes)

    mixed, grad_qkv, kept, given = call(
        attention_kernel,
        [
            low(own_cols, length),
            low(length, 3 * own_cols),
            low(n_chip, block_rows, block_cols),
            low(n_chip, block_rows, block_cols),
        ],
        [qkv, mixed_grad, *tables, first_turned, dy_low],
        14 * own_cols * length * length + 8 * own_cols * length * width,
        scratch=[
            pltpu.VMEM((own_heads, length, HD), wide_type),
            pltpu.VMEM((own_heads, length, HD), wide_type),
            pltpu.VMEM((width, block_cols), low_type),
            pltpu.VMEM((width, length), low_type),
            pltpu.VMEM((length, width), low_type),
            pltpu.SemaphoreType.DMA((2,)),
        ],
        flags=[core],
        far=(5, 6),
        name="attention",
    )
    grad_block = (kept.astype(wide_type) + swap(given).astype(wide_type)).astype(low_type)
    lane_block = (own_cols, length // steps), lambda step: (0, step)
    unit_block = (2, hidden_units // 2, length // steps), lambda step: (0, 0, step)
    branch, mark = call_rows(
        branch_kernel,
        [wide(length, width), wide(8, 128)],
        [hidden, mixed, ffn_all, w_out],
        [unit_block, lane_block, (down_view[0], lambda step: down_view[1]), None, row_block(width), None],
        2 * (own_cols + hidden_units) * length * width,
        steps,
        "branch",
    )
    grad_block, ffn_parts = lax.optimization_barrier((grad_block, ffn_parts))
    ffn_grad = jnp.sum(ffn_parts.astype(wide_type), axis=0).reshape(2, ffn_rows, width)
    grad_parts = trade(grad_block, chip_axes)
    grad_parts, mark = lax.optimization_barrier((grad_parts, mark))
    branch = lax.psum_scatter(branch, ctx_axes, scatter_dimension=0, tiled=True)
    grad_block = jnp.sum(grad_parts.astype(wide_type), axis=0)

    own, ffn_moment_new = call(
        owners_kernel,
        [low(n_chip, ffn_rows, width), wide(2, ffn_rows, width)],
        [ffn_moment, ffn_grad, moment_block, grad_block],
        0,
        name="owners",
    )
    own, grad_qkv = lax.optimization_barrier((own, grad_qkv))
    own = trade(own, chip_axes)
    grad_normed, vec_sums = call_rows(
        normal_kernel,
        [low(length, width), wide(4, width)],
        [grad_qkv, grad_up, first_pack, w_qkv, ffn_all, gain_one[None], gain_two[None]],
        [row_block(3 * own_cols), unit_block, x_rows, None, (up_view[0], lambda step: up_view[1])]
        + [None, None, row_block(width), None],
        2 * (3 * own_cols + hidden_units) * length * width,
        steps,
        "normal",
    )
    own, grad_normed, vec_sums = lax.optimization_barrier((own, grad_normed, vec_sums))
    own_block = own[:, :attn_rows].reshape(n_chip, attn_rows, n_ctx, own_cols).transpose(0, 2, 1, 3)
    own_block = own_block.reshape(width // 2, own_cols)
    own = own.reshape(n_chip * ffn_rows, width)
    owns_ffn = (chip == ffn_owners[0]) | (chip == ffn_owners[1])
    (gram,) = call(
        gram_kernel,
        [low(n_ctx, width // 2, own_cols)],
        [own, swap(own)],
        2 * own.shape[0] * width * width,
        flags=[core],
        name="gram",
    )
    gram = collect(gram, ctx_axes).astype(low_type)
    shard = jnp.where(owns_ffn, gram, own_block)

    own_x = inputs[0].astype(wide_type)
    own_dy = out_grad[0].astype(wide_type)
    bias_sums = jnp.sum(grad_qkv.astype(wide_type), axis=0)
    placed = [
        lax.dynamic_update_slice(
            jnp.zeros((width,), wide_type),
            bias_sums[index * own_cols : (index + 1) * own_cols],
            (ctx * own_cols,),
        )
        for index in range(3)
    ]
    grad_b_up = grad_b_up[:, 0].reshape(2, n_chip, ffn_rows).transpose(1, 0, 2)
    placed_up = lax.dynamic_update_slice(
        jnp.zeros((n_dp, n_ctx, ffn_rows), wide_type),
        grad_b_up.reshape(n_dp, 1, ffn_rows),
        (0, ctx, 0),
    ).reshape(-1)
    grad_bias_out = jnp.sum(own_dy, axis=0)
    vec_part = jnp.concatenate([vec_sums.reshape(-1), *placed, grad_bias_out, grad_bias_out, placed_up])
    vec_part = vec_part.reshape(n_dp, n_ctx, n_vec).transpose(1, 0, 2)
    vec_part = jnp.concatenate(split_low(vec_part), axis=2).reshape(n_ctx, -1)
    n_sent = vec_part.shape[1]
    vec_part = jnp.pad(vec_part, ((0, 0), (0, 4 * width - n_sent))).reshape(n_ctx, -1, own_cols)
    vec_lines = vec_part.shape[1]
    cols_send = jnp.concatenate(split_low(grad_block[:, : 3 * own_cols]), axis=1)
    cols_send = cols_send.reshape(n_ctx, attn_rows, 6 * own_cols)
    out_part = jnp.stack(split_low(grad_block[:, 3 * own_cols :]), axis=1)
    out_part = out_part.reshape(-1, 2, 2, n_ctx, attn_rows).transpose(3, 4, 2, 1, 0)
    out_part = out_part.reshape(n_ctx, attn_rows, 2 * own_cols)
    grad_send = jnp.concatenate([cols_send, out_part], axis=2).reshape(n_ctx, -1, own_cols)
    small_send = jnp.concatenate([vec_part, grad_send], axis=1)
    out_pack = grad_normed.reshape(n_ctx, own_len, width)
    out_pack, small_send, shard = lax.optimization_barrier((out_pack, small_send, shard))
    shard = jnp.broadcast_to(shard, (n_ctx,) + shard.shape)
    shard = trade(jnp.concatenate([shard, small_send], axis=1), ctx_axes)
    out_pack, shard = lax.optimization_barrier((out_pack, shard))
    other = swap(shard)
    out_pack = trade(out_pack, ctx_axes)

    (current,) = call(
        newton_schulz_kernel,
        [low(*own.shape)],
        [shard, other, own],
        20 * width * width * width,
        scratch=[
            pltpu.VMEM((width, width), wide_type),
            pltpu.VMEM((width, width), low_type),
            pltpu.VMEM((width, width), low_type),
            pltpu.VMEM((width, width), low_type),
            pltpu.VMEM(own.shape, wide_type),
        ],
        flags=[owns_ffn, core, ctx, chip == attn_owners[3]],
        name="newton_schulz",
    )
    small_sent, current = lax.optimization_barrier((shard[:, width // 2 :], current))
    out_sum = small_sent[:, :vec_lines].astype(wide_type).sum(axis=0)
    vec_sum = out_sum.reshape(-1)[:n_sent].reshape(n_chip, 2, 2, n_vec).sum(axis=2)
    vec_kept = lax.dynamic_index_in_dim(vec_sum, core, axis=1, keepdims=False)
    vec_given = lax.dynamic_index_in_dim(vec_sum, 1 - core, axis=1, keepdims=False)
    attn_grad = small_sent[:, vec_lines:].reshape(n_ctx, attn_rows, width).astype(wide_type)
    cols_grad = attn_grad[:, :, : 3 * own_cols] + attn_grad[:, :, 3 * own_cols : 6 * own_cols]
    cols_grad = cols_grad.reshape(n_ctx, attn_rows, 3, own_cols).transpose(2, 1, 0, 3)
    out_part = attn_grad[:, :, 6 * own_cols :].reshape(n_chip, attn_rows, 2, 2, -1).sum(axis=3)
    out_part = out_part.transpose(2, 0, 1, 3)
    out_kept = lax.dynamic_index_in_dim(out_part, core, axis=0, keepdims=False)
    out_given = lax.dynamic_index_in_dim(out_part, 1 - core, axis=0, keepdims=False)
    both = jnp.concatenate([vec_given, out_given.reshape(n_chip, -1)], axis=1)
    both = swap(both)
    vec_sum = vec_kept + both[:, :n_vec]
    out_part = pair(out_kept, both[:, n_vec:].reshape(out_given.shape)).transpose(1, 2, 0, 3)
    out_part = out_part.reshape(n_chip, attn_rows, own_cols)
    vec_row = jnp.concatenate(split_low(vec_sum), axis=1)
    vec_row = jnp.pad(vec_row[:, None], ((0, 0), (0, attn_rows - 1), (0, width - 2 * own_cols - 2 * n_vec)))
    last_rows = jnp.concatenate([*split_low(out_part), vec_row], axis=2)
    back = jnp.concatenate([current.reshape(n_chip, ffn_rows, width), last_rows], axis=1)
    back, out_pack = lax.optimization_barrier((back, out_pack))
    back = trade(back, chip_axes)
    grad_normed = jnp.sum(out_pack.astype(wide_type), axis=0)
    own_mean = jnp.mean(own_x, axis=-1, keepdims=True)
    own_centered = own_x - own_mean
    own_var = jnp.mean(own_centered * own_centered, axis=-1, keepdims=True)
    own_std = lax.rsqrt(own_var + norm_epsilon)
    own_normed = own_centered * own_std
    grad_center = (
        grad_normed
        - jnp.mean(grad_normed, axis=-1, keepdims=True)
        - own_normed * jnp.mean(grad_normed * own_normed, axis=-1, keepdims=True)
    )
    input_grad = (own_dy + own_std * grad_center)[None]
    outputs = (own_x + branch + bias_o + bias_down).astype(low_type)[None]
    back, input_grad, outputs = lax.optimization_barrier((back, input_grad, outputs))
    back = back.astype(wide_type)
    ortho_ffn = jnp.stack([back[owner, :ffn_rows] for owner in ffn_owners])
    ortho_attn = jnp.stack([back[owner, :attn_rows] for owner in attn_owners])
    last_rows = back[:, ffn_rows:]
    vec_grad = last_rows[:, 0, 2 * own_cols : 2 * own_cols + 2 * n_vec].reshape(n_chip, 2, n_vec)
    vec_grad = vec_grad.sum(axis=(0, 1))
    out_part = last_rows[:, :, :own_cols] + last_rows[:, :, own_cols : 2 * own_cols]
    out_part = out_part.transpose(1, 0, 2).reshape(1, attn_rows, width)
    attn_grad = jnp.concatenate([cols_grad.reshape(3, attn_rows, width), out_part], axis=0)
    attn_moment_new = momentum_decay * attn_moment + attn_grad
    attn_steps = jnp.array([1.0, 1.0, 1.0, 2.0], wide_type)
    ffn_steps = jnp.array([math.sqrt(FF / D), 2.0], wide_type)
    attn_new = (
        attn_weights * (1.0 - learn_rate * weight_decay)
        - learn_rate * attn_steps[:, None, None] * ortho_attn
    )
    ffn_new = (
        ffn_weights * (1.0 - learn_rate * weight_decay)
        - learn_rate * ffn_steps[:, None, None] * ortho_ffn
    )
    vec_first_new = beta_first * vec_first + (1.0 - beta_first) * vec_grad
    vec_second_new = beta_second * vec_second + (1.0 - beta_second) * vec_grad * vec_grad
    first_hat = vec_first_new / (1.0 - beta_first**STEP)
    second_hat = vec_second_new / (1.0 - beta_second**STEP)
    vec_new = vectors - vector_rate * first_hat / (jnp.sqrt(second_hat) + adam_epsilon)
    return (
        outputs,
        input_grad,
        attn_grad,
        ffn_grad,
        vec_grad,
        attn_moment_new,
        ffn_moment_new,
        attn_new,
        ffn_new,
        vec_first_new,
        vec_second_new,
        vec_new,
    )


def solution(mesh):
    names = dp_axes + ctx_axes
    fine = Mesh(mesh.devices.reshape(2, 4, 2, 2, 4), names)
    in_specs = (
        P(dp_axes, ctx_axes, None),
        P(dp_axes, ctx_axes, None),
        P(None, dp_axes + ctx_axes, None),
        P(None, dp_axes + ctx_axes, None),
        P(dp_axes + ctx_axes),
        P(None, dp_axes + ctx_axes, None),
        P(None, dp_axes + ctx_axes, None),
        P(dp_axes + ctx_axes),
        P(dp_axes + ctx_axes),
    )
    out_specs = (
        P(dp_axes, ctx_axes, None),
        P(dp_axes, ctx_axes, None),
        P(None, dp_axes + ctx_axes, None),
        P(None, dp_axes + ctx_axes, None),
        P(dp_axes + ctx_axes),
        P(None, dp_axes + ctx_axes, None),
        P(None, dp_axes + ctx_axes, None),
        P(None, dp_axes + ctx_axes, None),
        P(None, dp_axes + ctx_axes, None),
        P(dp_axes + ctx_axes),
        P(dp_axes + ctx_axes),
        P(dp_axes + ctx_axes),
    )
    return jax.shard_map(local, mesh=fine, in_specs=in_specs, out_specs=out_specs, check_vma=False)
```
